256 devices in a mesh: pipe: 2 (over core), dp: 32 (over z, x), tensor: 4 (over y).
Axes of the slice: x: 4, y: 4, z: 8, core: 2. Of those that a mesh axis runs over, the one named last changes fastest.
Arguments:
- text_embeds: bfloat16 [64, 128, 4096], P('dp', None, 'tensor'), may hold values from -10 to 10
- patches: bfloat16 [64, 64, 3200], P('dp', 'pipe'), may hold values from -6 to 6
- image_tokens: int32 [64], P('dp'), may hold values from 1 to 64, 2048 in all
- connector: bfloat16 [3200, 4096], P('dp', 'tensor'), may hold values from -0.109375 to 0.109375
- w_query: bfloat16 [2, 4096, 4096], P('pipe', 'dp', 'tensor'), may hold values from -2 to 2
- w_keyval: bfloat16 [2, 2, 4096, 1024], P('pipe', None, 'dp', 'tensor'), may hold values from -2 to 2
- w_out: bfloat16 [2, 4096, 4096], P('pipe', 'tensor', 'dp'), may hold values from -0.09375 to 0.09375
Outputs:
- final_hidden: bfloat16 [64, 128, 4096], P('dp', 'pipe', 'tensor')
The draws below stay inside these ranges and needn't reach their ends.
Inputs may be any that keep to these rules, and one draw needn't show every extreme that they name: Sequence b holds image tokens at its first image_tokens[b] positions; some sequence reaches 64.
All inputs are finite; a program needn't handle non-finite values. No bound on the sum of `image_tokens` on one device may be relied on, other than what follows from the above.
Results may differ from the reference program's by a relative error of at most 0.01.
Values may be sent and summed in bfloat16 or wider, within the bound.
A program may use at most 128 MiB of HBM per device.

```python
import math
import jax
import jax.numpy as jnp
import numpy as np
from jax import lax

D = 4096
HEADS = 32
KV_HEADS = 8
HEAD = 128
VIT = 3200
SEQ = 128
MB = 2
IMG_MAX = 64
QW = 4096
KVW = 1024
SECTIONS = 2
DP_MB = 64
N_DP = 32


def draw_text_embeds(key, part):
    key = jax.random.fold_in(key, 1)
    drawn = jax.random.truncated_normal(jax.random.fold_in(key, 11), -6.0, 6.0, (DP_MB, SEQ, D), jnp.float32)
    return drawn.astype(jnp.bfloat16)


def draw_w_query(key, part):
    key = jax.random.fold_in(key, 2)
    drawn = jax.random.truncated_normal(jax.random.fold_in(key, 21), -6.0, 6.0, (SECTIONS, D, QW), jnp.float32) / math.sqrt(D)
    return drawn.astype(jnp.bfloat16)


def draw_w_keyval(key, part):
    key = jax.random.fold_in(key, 3)
    drawn = jax.random.truncated_normal(jax.random.fold_in(key, 31), -6.0, 6.0, (SECTIONS, 2, D, KVW), jnp.float32) / math.sqrt(D)
    return drawn.astype(jnp.bfloat16)


def block_scale(stream_key, shape, pieces, low, top_value):
    def one(axis_at, blocks):
        draws = jax.random.uniform(jax.random.fold_in(jax.random.fold_in(stream_key, 6), axis_at), (blocks,), jnp.float32, low / len(pieces), top_value / len(pieces))
        return jnp.repeat(jnp.exp(draws), shape[axis_at] // blocks).reshape((-1,) + (1,) * (len(shape) - axis_at - 1))

    gain = one(*pieces[0])
    for cut in pieces[1:]:
        gain = gain * one(*cut)
    return gain


def length_profile(count, total, reach, slope):
    portions = [(1 << 20) // math.isqrt(standing ** slope) + 1 for standing in range(2, count + 1)]
    spare, holding = total - reach - (count - 1), [1] * (count - 1)
    while spare > 0:
        free = [i for i in range(count - 1) if holding[i] < reach]
        pool, left = sum([portions[i] for i in free]), spare
        for i in free:
            addition = min(reach - holding[i], max(1, left * portions[i] // pool), spare)
            holding[i] = holding[i] + addition
            spare = spare - addition
    return np.array([reach] + holding)


def uneven_parts(own_key, amount, total, bound, skew):
    if amount == 2:
        one = jax.random.randint(own_key, (), max(1, total - bound), min(bound, total - 1) + 1)
        return jnp.stack([one, total - one])
    lengths = jnp.asarray(length_profile(amount, total, bound, skew), jnp.int32)
    couples = (amount - 1) // 2
    donor, receiver = lengths[1:1 + 2 * couples:2], lengths[2:2 + 2 * couples:2]
    slack = jnp.minimum(donor - 1, bound - receiver)
    shifted = jax.random.randint(jax.random.fold_in(own_key, 1), (couples,), 0, 1 << 20) % (slack + 1)
    lengths = lengths.at[1:1 + 2 * couples:2].set(donor - shifted).at[2:2 + 2 * couples:2].set(receiver + shifted)
    return lengths[jax.random.permutation(jax.random.fold_in(own_key, 2), amount)]


def normal_values(rng, dims, spread, bound, split=(), kind=jnp.bfloat16):
    factor_of = block_scale(rng, dims, split, -0.22, 0.18) if split else 1.0
    values = jax.random.normal(rng, dims, jnp.float32) * spread * factor_of
    return jnp.minimum(jnp.maximum(values, -bound), bound).astype(kind)


def setup_inputs(seed: int = 0) -> dict:
    key_of = jax.random.split(jax.random.key(seed), 8)
    text_embeds = draw_text_embeds(jax.random.fold_in(key_of[7], 71), 0)
    patches = normal_values(key_of[1], (DP_MB, IMG_MAX, VIT), 1.0, 6.0, ((0, 32), (1, 2)))
    image_tokens = uneven_parts(key_of[2], DP_MB, MB * N_DP * IMG_MAX // 2, IMG_MAX, 2).astype(jnp.int32)
    connector = normal_values(key_of[3], (VIT, D), VIT ** -0.5, 0.109375, ((0, 32), (1, 4)))
    w_query = draw_w_query(jax.random.fold_in(key_of[7], 71), 0)
    w_keyval = draw_w_keyval(jax.random.fold_in(key_of[7], 71), 0)
    w_out = normal_values(key_of[6], (SECTIONS, QW, D), QW ** -0.5, 0.09375, ((0, 2), (1, 4), (2, 32)))
    return dict(text_embeds=text_embeds, patches=patches, image_tokens=image_tokens, connector=connector, w_query=w_query, w_keyval=w_keyval, w_out=w_out)


def rotate(values, positions):
    half_size = values.shape[-1] // 2
    frequencies = 500000.0 ** (-(jnp.arange(half_size, dtype=jnp.float32) * 2.0 / values.shape[-1]))
    angles = positions.astype(jnp.float32)[:, None] * frequencies[None, :]
    cosine = jnp.cos(angles)[:, None, :]
    sine_part = jnp.sin(angles)[:, None, :]
    lower_half = values[..., :half_size]
    upper_half = values[..., half_size:]
    return jnp.concatenate([lower_half * cosine - upper_half * sine_part, upper_half * cosine + lower_half * sine_part], axis=-1)

def project_patches(patches, connector):
    values = patches.astype(jnp.float32)
    centered = values - lax.optimization_barrier(jnp.mean(values, axis=-1, keepdims=True))
    normed = (centered * lax.rsqrt(lax.optimization_barrier(jnp.mean(centered * centered, axis=-1, keepdims=True)) + 1e-06)).astype(jnp.bfloat16)
    return jnp.einsum('bpv,vd->bpd', normed.astype(jnp.float32), connector.astype(jnp.float32)).astype(jnp.bfloat16)

def decoder_attention(hidden, w_query, w_keyval, w_out):
    batches, length, width = hidden.shape
    values = hidden.astype(jnp.float32)
    normed = (values * lax.rsqrt(lax.optimization_barrier(jnp.mean(values * values, axis=-1, keepdims=True)) + 1e-05)).astype(jnp.bfloat16)
    normed_wide = normed.astype(jnp.float32)
    queries = jnp.einsum('bsd,dk->bsk', normed_wide, w_query.astype(jnp.float32))
    keyval = jnp.einsum('bsd,jdk->jbsk', normed_wide, w_keyval.astype(jnp.float32))
    positions = jnp.arange(length)
    queries = rotate(queries.reshape(batches, length, HEADS, HEAD), positions).astype(jnp.bfloat16)
    key_rows = rotate(keyval[0].reshape(batches, length, KV_HEADS, HEAD), positions).astype(jnp.bfloat16)
    value_rows = keyval[1].reshape(batches, length, KV_HEADS, HEAD).astype(jnp.bfloat16)
    group_size = HEADS // KV_HEADS
    queries = queries.reshape(batches, length, KV_HEADS, group_size, HEAD)
    scores = jnp.einsum('bsgqe,btge->bgqst', queries.astype(jnp.float32), key_rows.astype(jnp.float32)) / math.sqrt(HEAD)
    causal = positions[:, None] >= positions[None, :]
    scores = jnp.where(causal, scores, -1e+30)
    scores = scores - lax.optimization_barrier(jnp.max(scores, axis=-1, keepdims=True))
    weights = jnp.exp(scores)
    probabilities = (weights / lax.optimization_barrier(jnp.sum(weights, axis=-1, keepdims=True))).astype(jnp.bfloat16)
    attended = jnp.einsum('bgqst,btge->bsgqe', probabilities.astype(jnp.float32), value_rows.astype(jnp.float32)).astype(jnp.bfloat16)
    attended = attended.reshape(batches, length, HEADS * HEAD)
    update = jnp.einsum('bsk,kd->bsd', attended.astype(jnp.float32), w_out.astype(jnp.float32))
    return (values + update).astype(jnp.bfloat16)

def reference(text_embeds, patches, image_tokens, connector, w_query, w_keyval, w_out):
    image_rows = project_patches(patches, connector)
    length = text_embeds.shape[1]
    padded = jnp.pad(image_rows, ((0, 0), (0, length - image_rows.shape[1]), (0, 0)))
    inside = jnp.arange(length)[None, :] < image_tokens[:, None]
    hidden = jnp.where(inside[:, :, None], padded, text_embeds)
    for section_number in range(w_query.shape[0]):
        hidden = decoder_attention(hidden, w_query[section_number], w_keyval[section_number], w_out[section_number])
    return hidden
```

```python
import math

import jax
import jax.numpy as jnp
import numpy as np
from jax import lax
from jax.experimental import pallas as pl
from jax.experimental.pallas import tpu as pltpu
from jax.sharding import PartitionSpec as P

MESH = pl.DeviceIdType.MESH
BF = jnp.bfloat16
F32 = jnp.float32
NX, NY, NZ = 4, 4, 8
SCALE = 1.0 / math.sqrt(128)

RING = [
    (0, 1), (1, 1), (0, 2), (2, 1), (0, 3), (1, 2), (0, 4), (1, 3), (0, 5),
    (2, 2), (1, 4), (2, 3), (1, 5), (3, 1), (2, 4), (3, 2), (2, 5),
    (4, 1), (3, 3), (4, 2), (3, 4), (4, 3), (3, 5), (4, 4), (4, 5),
]


def remote(src, dst, send_sem, recv_sem, device):
    return pltpu.make_async_remote_copy(
        src_ref=src,
        dst_ref=dst,
        send_sem=send_sem,
        recv_sem=recv_sem,
        device_id=device,
        device_id_type=MESH,
    )


def kernel(
    text, patches, tokens, conn, wq, wkv, wo, cosine, sine, out,
    CN, WQ, WO, PNS, PN, TS, T0, IS, IR, H, QS, QR, AR, OS, OR, FS, FR,
    own_s, own_r, z_s, z_r, f_s, f_r, p_s, p_r, t_s, t_r, i_s, i_r,
    h_s, h_r, q_s, q_r, a_s, a_r, o_s, o_r, e_s, e_r,
):
    c = lax.axis_index("pipe")
    d = lax.axis_index("dp")
    y = lax.axis_index("tensor")
    z = lax.div(d, NX)
    x = lax.rem(d, NX)

    def at(core, zz, xx, yy):
        return (core, zz * NX + xx, yy)

    def xk(k):
        return lax.rem(x + k, NX)

    def yk(k):
        return lax.rem(y + k, NY)

    def zk(k):
        return lax.rem(z + k + NZ, NZ)

    barrier = pltpu.get_barrier_semaphore()
    greeted = [at(1 - c, z, xk(k), y) for k in range(4)]
    greeted += [at(c, z, xk(k), y) for k in range(1, 4)]
    greeted += [at(c, z, x, yk(k)) for k in range(1, 4)]
    greeted += [at(c, zk(1), x, y), at(c, zk(-1), x, y)]
    for device in greeted:
        pl.semaphore_signal(barrier, inc=1, device_id=device, device_id_type=MESH)
    pl.semaphore_wait(barrier, len(greeted))

    zrow = pl.multiple_of(z * 128, 128)
    WQ[c, pl.ds(zrow, 128), pl.ds(0, 1024)] = wq[0]
    WQ[c, pl.ds(zrow, 128), pl.ds(1024, 256)] = wkv[0, 0]
    WQ[c, pl.ds(zrow, 128), pl.ds(1280, 256)] = wkv[0, 1]
    WO[c, :, pl.ds(zrow, 128)] = wo[0]
    CN[z, pl.ds(0, 112)] = conn[pl.ds(0, 112)]

    def block(item, zz, part):
        if item == 0:
            start, size = ((0, 112), (0, 64), (64, 48))[part]
            return CN.at[zz, pl.ds(start, size)]
        s = (item - 1) // 2
        if item % 2 == 1:
            start, size = ((0, 128), (0, 64), (64, 64))[part]
            return WQ.at[s, pl.ds(pl.multiple_of(zz * 128 + start, 64), size)]
        start, size = ((0, 1024), (0, 512), (512, 512))[part]
        return WO.at[s, pl.ds(start, size), pl.ds(pl.multiple_of(zz * 128, 128), 128)]

    def own_copy(s, n):
        ref = block(1 + 2 * s + n, z, 0)
        return remote(ref, ref, own_s.at[n], own_r.at[n], at(1 - s, z, x, y))

    def ring_send(item, step, way):
        zz = zk(1 - step) if way == 0 else zk(step - 1)
        ref = block(item, zz, 0 if step < 4 else 1 + way)
        target = at(1, zk(1) if way == 0 else zk(-1), x, y)
        return remote(ref, ref, z_s.at[item, step - 1, way], z_r.at[item, step - 1, way], target)

    def ring_arrival(item, step, way):
        zz = zk(-step) if way == 0 else zk(step)
        ref = block(item, zz, 0 if step < 4 else 1 + way)
        return remote(ref, ref, z_s.at[item, step - 1, way], z_r.at[item, step - 1, way], at(0, z, x, y))

    def hand_over(item, index):
        step = index // 2 + 1
        zz = zk(-step) if index % 2 == 0 else zk(step)
        ref = block(item, zz, 0)
        return remote(ref, ref, f_s.at[item, index], f_r.at[item, index], at(0, z, x, y))

    def patch_copy(k):
        return remote(PNS.at[xk(k)], PN.at[x, :, c], p_s.at[k], p_r.at[x, c], at(0, z, xk(k), y))

    def patch_arrival(source, core):
        ref = PN.at[source, :, core]
        return remote(ref, ref, p_s.at[0], p_r.at[source, core], at(0, z, x, y))

    def normed_patches():
        values = patches[...].reshape(64, 3200).astype(F32)
        centered = values - jnp.sum(values, axis=-1, keepdims=True) / 3200.0
        variance = jnp.sum(centered * centered, axis=-1, keepdims=True) / 3200.0
        normed = centered * lax.rsqrt(variance + 1e-06)
        row = lax.broadcasted_iota(jnp.int32, (64, 1), 0)
        limit = jnp.where(row < 32, tokens[0], tokens[1])
        normed = jnp.where(c * 32 + lax.rem(row, 32) < limit, normed, 0.0)
        lane = lax.broadcasted_iota(jnp.int32, (64, 128), 1)
        for j in range(32):
            zz, xx = divmod(j, NX)
            base = (100 * j) // 128 * 128
            offset = 100 * j - base
            width = 128 if offset + 100 <= 128 else 256
            window = normed[:, base : base + width]
            if offset:
                window = pltpu.roll(window, width - offset, 1)
            part = jnp.where(lane < 100, window[:, :128], 0.0)
            PNS[xx, :, :, zz * 128 : (zz + 1) * 128] = part.astype(BF).reshape(2, 32, 128)

    @pl.when(c == 1)
    def _():
        own = [own_copy(1, 0), own_copy(1, 1)]
        for copy in own:
            copy.start()
        ring_send(0, 1, 0).start()
        ring_send(0, 1, 1).start()
        normed_patches()
        for k in range(4):
            patch_copy(k).start()
        for item, step in RING[1:]:
            if step > 1:
                ring_arrival(item, step - 1, 0).wait_recv()
                ring_arrival(item, step - 1, 1).wait_recv()
            elif item in (1, 2):
                own_copy(0, item - 1).wait_recv()
            if step < 5:
                ring_send(item, step, 0).start()
                ring_send(item, step, 1).start()
            if step > 1:
                for index in (6,) if step == 5 else (2 * step - 4, 2 * step - 3):
                    hand_over(item, index).start()
        for copy in own:
            copy.wait_send()
        for k in range(4):
            patch_copy(k).wait_send()
        for item in range(5):
            for step in range(1, 5):
                for way in range(2):
                    ring_send(item, step, way).wait_send()
            for index in range(7):
                hand_over(item, index).wait_send()

    def wait_item(item):
        for index in range(7):
            hand_over(item, index).wait_recv()

    def text_copy(half, k):
        target = at(0, z, xk(k), y)
        if half == 1:
            return remote(TS.at[xk(k), :, 1], H.at[0, :, 1, y, x], t_s.at[1, k], t_r.at[1, x], target)
        return remote(TS.at[xk(k), :, 0], T0.at[:, x], t_s.at[0, k], t_r.at[0, x], target)

    def text_arrival(half, k):
        ref = H.at[0, :, 1, y, xk(k)] if half == 1 else T0.at[:, xk(k)]
        return remote(ref, ref, t_s.at[half, k], t_r.at[half, xk(k)], at(1, z, x, y))

    def image_copy(k):
        return remote(IS.at[xk(k)], IR.at[x], i_s.at[k], i_r.at[x], at(0, z, xk(k), y))

    def image_arrival(k):
        ref = IR.at[xk(k)]
        return remote(ref, ref, i_s.at[k], i_r.at[xk(k)], at(1, z, x, y))

    def hidden_copy(s, b, h, k):
        ref = H.at[s, b, h, y]
        return remote(ref, ref, h_s.at[s, b, h, k], h_r.at[s, b, h, y], at(0, z, x, yk(k)))

    def hidden_arrival(s, b, h, k):
        ref = H.at[s, b, h, yk(k)]
        return remote(ref, ref, h_s.at[s, b, h, k], h_r.at[s, b, h, yk(k)], at(1, z, x, y))

    def qkv_copy(s, b, h, k):
        return remote(
            QS.at[s, b, h, xk(k)], QR.at[s, b, h, x], q_s.at[s, b, h, k], q_r.at[s, b, h, x], at(0, z, xk(k), y)
        )

    def qkv_arrival(s, b, h, k):
        ref = QR.at[s, b, h, xk(k)]
        return remote(ref, ref, q_s.at[s, b, h, k], q_r.at[s, b, h, xk(k)], at(1, z, x, y))

    def attended_copy(s, b, k):
        ref = AR.at[s, b, x]
        return remote(ref, ref, a_s.at[s, b, k], a_r.at[s, b, x], at(0, z, xk(k), y))

    def attended_arrival(s, b, k):
        ref = AR.at[s, b, xk(k)]
        return remote(ref, ref, a_s.at[s, b, k], a_r.at[s, b, xk(k)], at(1, z, x, y))

    def update_copy(s, b, k):
        return remote(OS.at[s, b, yk(k)], OR.at[s, b, y], o_s.at[s, b, k], o_r.at[s, b, y], at(0, z, x, yk(k)))

    def update_arrival(s, b, k):
        ref = OR.at[s, b, yk(k)]
        return remote(ref, ref, o_s.at[s, b, k], o_r.at[s, b, yk(k)], at(1, z, x, y))

    def final_copy(b, h, k):
        return remote(FS.at[b, h, xk(k)], FR.at[x, b], e_s.at[b, h, k], e_r.at[x, b], at(h, z, xk(k), y))

    def final_arrival(b, k):
        ref = FR.at[xk(k), b]
        return remote(ref, ref, e_s.at[b, 0, k], e_r.at[xk(k), b], at(1 - c, z, x, y))

    def send_text():
        position = lax.broadcasted_iota(jnp.int32, (128, 1), 0)
        for b in range(2):
            masked = jnp.where(position < tokens[b], jnp.zeros_like(text[b]), text[b])
            for xx in range(NX):
                for zz in range(2):
                    lanes = zz * 512 + xx * 128
                    TS[xx, b, :, :, zz * 128 : (zz + 1) * 128] = masked[:, lanes : lanes + 128].reshape(2, 64, 128)
        for b in range(2):
            H[0, b, 1, y, x] = TS[x, b, 1]
            T0[b, x] = TS[x, b, 0]
        for half in (1, 0):
            for k in range(1, 4):
                text_copy(half, k).start()

    def image_part():
        for core in range(2):
            for k in range(1 - core, 4):
                patch_arrival(xk(k), core).wait_recv()
        wait_item(0)
        rows = PN[...].reshape(512, 1024)
        for zz in range(2):
            for pair in range(2):
                lanes = zz * 512 + pair * 256
                product = jnp.dot(
                    rows, CN[:, :, lanes : lanes + 256].reshape(1024, 256), preferred_element_type=F32
                ).astype(BF)
                for n in range(2):
                    IS[2 * pair + n, :, :, :, zz * 128 : (zz + 1) * 128] = product[:, n * 128 : (n + 1) * 128].reshape(
                        4, 2, 64, 128
                    )
        for k in range(1, 4):
            image_copy(k).start()
        for k in range(1, 4):
            text_arrival(0, k).wait_recv()
        for k in range(1, 4):
            image_arrival(k).wait_recv()
        for b in range(2):
            total = IS[x, :, b].astype(F32)
            for k in range(1, 4):
                total = total + IR[xk(k), :, b].astype(F32)
            H[0, b, 0, y] = (total.astype(BF).astype(F32) + T0[b].astype(F32)).astype(BF)
            for k in range(1, 4):
                hidden_copy(0, b, 0, k).start()

    def project(s, b, h):
        squares = jnp.zeros((256, 256), F32)
        for q in range(4):
            values = H[s, b, h, q].reshape(256, 256).astype(F32)
            squares = squares + values * values
        squares = jnp.sum(squares, axis=-1, keepdims=True)
        high = squares.astype(BF).astype(F32)
        lane = lax.broadcasted_iota(jnp.int32, (256, 128), 1)
        QS[s, b, h, :, :, 1536:1664] = (
            jnp.where(lane < 64, high, squares - high).astype(BF).reshape(4, 64, 128)
        )

        def tile(n, _):
            lanes = pl.ds(pl.multiple_of(n * 256, 256), 256)
            total = jnp.zeros((256, 256), F32)
            for q in range(4):
                total = total + jnp.dot(
                    H[s, b, h, q].reshape(256, 256),
                    WQ[s, pl.ds(q * 256, 256), lanes],
                    preferred_element_type=F32,
                )
            QS[s, b, h, :, :, lanes] = total.astype(BF).reshape(4, 64, 256)
            return 0

        lax.fori_loop(0, 6, tile, 0)
        for k in range(1, 4):
            qkv_copy(s, b, h, k).start()

    def attend(s, b):
        queries = [[None] * 8, [None] * 8]
        keys = [[None] * 2, [None] * 2]
        values = [[None] * 2, [None] * 2]
        for h in range(2):
            for k in range(1, 4):
                qkv_arrival(s, b, h, k).wait_recv()

            def summed(start):
                lanes = slice(start, start + 128)
                total = QS[s, b, h, x, :, lanes].astype(F32)
                for k in range(1, 4):
                    total = total + QR[s, b, h, xk(k), :, lanes].astype(F32)
                return total

            squares = summed(1536)
            scale = lax.rsqrt((squares[:, 0:1] + squares[:, 64:65]) / 4096.0 + 1e-05)
            cos_rows = cosine[h * 64 : (h + 1) * 64]
            sin_rows = sine[h * 64 : (h + 1) * 64]

            def rotated(start):
                rows = summed(start) * scale
                return (rows * cos_rows + pltpu.roll(rows, 64, 1) * sin_rows).astype(BF)

            for j in range(8):
                queries[h][j] = rotated(j * 128)
            for g in range(2):
                keys[h][g] = rotated(1024 + g * 128)
                values[h][g] = (summed(1280 + g * 128) * scale).astype(BF)
        row = lax.rem(lax.broadcasted_iota(jnp.int32, (512, 128), 0), 128)
        column = lax.broadcasted_iota(jnp.int32, (512, 128), 1)
        for g in range(2):
            stacked = jnp.concatenate([queries[h][4 * g + j] for j in range(4) for h in range(2)], axis=0)
            key_rows = jnp.concatenate([keys[0][g], keys[1][g]], axis=0)
            value_rows = jnp.concatenate([values[0][g], values[1][g]], axis=0)
            scores = lax.dot_general(
                stacked, key_rows, (((1,), (1,)), ((), ())), preferred_element_type=F32
            )
            scores = jnp.where(row >= column, scores * SCALE, -1e30)
            weights = jnp.exp(scores - jnp.max(scores, axis=-1, keepdims=True))
            norm = jnp.sum(weights, axis=-1, keepdims=True)
            mixed = jnp.dot(weights.astype(BF), value_rows, preferred_element_type=F32) / norm
            for j in range(4):
                lanes = (4 * g + j) * 128
                AR[s, b, x, :, lanes : lanes + 128] = mixed[j * 128 : (j + 1) * 128].astype(BF)
        for k in range(1, 4):
            attended_copy(s, b, k).start()

    def update(s, b):
        for k in range(1, 4):
            attended_arrival(s, b, k).wait_recv()

        def tile(n, _):
            yd = yk(n + 1)
            lanes = pl.ds(pl.multiple_of(yd * 256, 256), 256)
            product = jnp.dot(AR[s, b].reshape(512, 1024), WO[s, :, lanes], preferred_element_type=F32)
            OS[s, b, yd] = product.astype(BF).reshape(4, 2, 64, 256)

            @pl.when(n < 3)
            def _():
                update_copy(s, b, n + 1).start()

            return 0

        lax.fori_loop(0, 4, tile, 0)

    def renew(s, b):
        for k in range(1, 4):
            update_arrival(s, b, k).wait_recv()
        for h in range(2):
            total = OS[s, b, y, :, h].astype(F32)
            for k in range(1, 4):
                total = total + OR[s, b, yk(k), :, h].astype(F32)
            fresh = (H[s, b, h, y].astype(F32) + total).astype(BF)

            @pl.when(s == 0)
            def _():
                H[1, b, h, y] = fresh
                for k in range(1, 4):
                    hidden_copy(1, b, h, k).start()

            @pl.when(s == 1)
            def _():
                FS[b, h] = fresh
                for k in range(1 - h, 4):
                    final_copy(b, h, k).start()

    @pl.when(c == 0)
    def _():
        own_copy(0, 0).start()
        own_copy(0, 1).start()
        send_text()
        for zz in range(NZ):
            CN[zz, pl.ds(112, 16)] = jnp.zeros((16, 1024), BF)
        normed_patches()
        PN[x, :, 0] = PNS[x]
        for k in range(1, 4):
            patch_copy(k).start()
        for k in range(1, 4):
            text_arrival(1, k).wait_recv()
        for b in range(2):
            for k in range(1, 4):
                hidden_copy(0, b, 1, k).start()
        image_part()

        def section(s, _):
            @pl.when(s == 0)
            def _():
                wait_item(1)

            @pl.when(s == 1)
            def _():
                own_copy(1, 0).wait_recv()
                wait_item(3)

            def unit(u, _):
                outer, inner = lax.div(u, 2), lax.rem(u, 2)
                b = jnp.where(s == 0, inner, outer)
                h = jnp.where(s == 0, 1 - outer, inner)
                for k in range(1, 4):
                    hidden_arrival(s, b, h, k).wait_recv()
                project(s, b, h)
                return 0

            def attention(b, _):
                attend(s, b)
                return 0

            def output(b, _):
                update(s, b)
                return 0

            def residual(b, _):
                renew(s, b)
                return 0

            lax.fori_loop(0, 4, unit, 0)
            lax.fori_loop(0, 2, attention, 0)

            @pl.when(s == 0)
            def _():
                wait_item(2)

            @pl.when(s == 1)
            def _():
                own_copy(1, 1).wait_recv()
                wait_item(4)

            lax.fori_loop(0, 2, output, 0)
            lax.fori_loop(0, 2, residual, 0)
            return 0

        lax.fori_loop(0, 2, section, 0)
        for b in range(2):
            FR[x, b] = FS[b, 0, x]

    for b in range(2):

        @pl.when(c == 1)
        def _():
            final_arrival(b, 0).wait_recv()

        for k in range(1, 4):
            final_arrival(b, k).wait_recv()
    for b in range(2):
        for xx in range(NX):
            for zz in range(2):
                lanes = zz * 512 + xx * 128
                out[b, :, lanes : lanes + 128] = FR[xx, b, :, zz * 128 : (zz + 1) * 128]

    @pl.when(c == 0)
    def _():
        own_copy(0, 0).wait_send()
        own_copy(0, 1).wait_send()
        for k in range(1, 4):
            patch_copy(k).wait_send()
            text_copy(0, k).wait_send()
            text_copy(1, k).wait_send()
            image_copy(k).wait_send()

        def drain(n, _):
            s, b = lax.div(n, 2), lax.rem(n, 2)
            for k in range(1, 4):
                for h in range(2):
                    hidden_copy(s, b, h, k).wait_send()
                    qkv_copy(s, b, h, k).wait_send()
                attended_copy(s, b, k).wait_send()
                update_copy(s, b, k).wait_send()
            return 0

        lax.fori_loop(0, 4, drain, 0)
        for b in range(2):
            for h in range(2):
                for k in range(1 - h, 4):
                    final_copy(b, h, k).wait_send()


def rotation_tables():
    frequencies = 500000.0 ** (-(np.arange(64, dtype=np.float32) * np.float32(2.0) / np.float32(128)))
    angles = np.arange(128, dtype=np.float32)[:, None] * frequencies.astype(np.float32)[None, :]
    cosine, sine = np.cos(angles), np.sin(angles)
    return (
        np.concatenate([cosine, cosine], axis=1).astype(np.float32),
        np.concatenate([-sine, sine], axis=1).astype(np.float32),
    )


def shards(text_embeds, patches, image_tokens, connector, w_query, w_keyval, w_out):
    cosine, sine = rotation_tables()
    padded = jnp.pad(connector, ((0, 12), (0, 0)))
    vmem = pl.BlockSpec(memory_space=pltpu.VMEM)
    dma = pltpu.SemaphoreType.DMA
    return pl.pallas_call(
        kernel,
        out_shape=jax.ShapeDtypeStruct((2, 64, 1024), BF),
        in_specs=[vmem, vmem, pl.BlockSpec(memory_space=pltpu.SMEM)] + [vmem] * 6,
        out_specs=vmem,
        scratch_shapes=[
            pltpu.VMEM((8, 128, 1024), BF),
            pltpu.VMEM((2, 1024, 1536), BF),
            pltpu.VMEM((2, 1024, 1024), BF),
            pltpu.VMEM((4, 2, 32, 1024), BF),
            pltpu.VMEM((4, 2, 2, 32, 1024), BF),
            pltpu.VMEM((4, 2, 2, 64, 256), BF),
            pltpu.VMEM((2, 4, 64, 256), BF),
            pltpu.VMEM((4, 4, 2, 64, 256), BF),
            pltpu.VMEM((4, 4, 2, 64, 256), BF),
            pltpu.VMEM((2, 2, 2, 4, 4, 64, 256), BF),
            pltpu.VMEM((2, 2, 2, 4, 64, 1664), BF),
            pltpu.VMEM((2, 2, 2, 4, 64, 1664), BF),
            pltpu.VMEM((2, 2, 4, 128, 1024), BF),
            pltpu.VMEM((2, 2, 4, 4, 2, 64, 256), BF),
            pltpu.VMEM((2, 2, 4, 4, 2, 64, 256), BF),
            pltpu.VMEM((2, 2, 4, 64, 256), BF),
            pltpu.VMEM((4, 2, 64, 256), BF),
            dma((2,)), dma((2,)),
            dma((5, 4, 2)), dma((5, 4, 2)),
            dma((5, 7)), dma((5, 7)),
            dma((4,)), dma((4, 2)),
            dma((2, 4)), dma((2, 4)),
            dma((4,)), dma((4,)),
            dma((2, 2, 2, 4)), dma((2, 2, 2, 4)),
            dma((2, 2, 2, 4)), dma((2, 2, 2, 4)),
            dma((2, 2, 4)), dma((2, 2, 4)),
            dma((2, 2, 4)), dma((2, 2, 4)),
            dma((2, 2, 4)), dma((4, 2)),
        ],
        compiler_params=pltpu.CompilerParams(
            collective_id=0, has_side_effects=True, vmem_limit_bytes=62 * 2**20
        ),
        cost_estimate=pl.CostEstimate(flops=11 * 10**9, bytes_accessed=20 * 10**6, transcendentals=10**6),
        name="decoder",
    )(text_embeds, patches, image_tokens, padded, w_query, w_keyval, w_out, cosine, sine)


def solution(mesh):
    placed = (
        P("dp", None, "tensor"),
        P("dp", "pipe", None),
        P("dp"),
        P("dp", "tensor"),
        P("pipe", "dp", "tensor"),
        P("pipe", None, "dp", "tensor"),
        P("pipe", "tensor", "dp"),
    )
    return jax.shard_map(
        shards, mesh=mesh, in_specs=placed, out_specs=P("dp", "pipe", "tensor"), check_vma=False
    )
```

```python
import math

import jax
import jax.numpy as jnp
import numpy as np
from jax import lax
from jax.experimental import pallas as pl
from jax.experimental.pallas import tpu as pltpu
from jax.sharding import PartitionSpec as P

MESH = pl.DeviceIdType.MESH
BF = jnp.bfloat16
F32 = jnp.float32
NX, NY, NZ = 4, 4, 8
SCALE = 1.0 / math.sqrt(128)

RING = [
    (0, 2), (0, 3), (0, 4), (1, 1), (0, 5), (1, 2), (1, 3), (1, 4), (2, 1), (1, 5), (2, 2), (2, 3), (3, 1), (2, 4), (2, 5),
    (3, 2), (3, 3), (3, 4), (4, 1), (3, 5), (4, 2), (4, 3), (4, 4), (4, 5),
]
PIECES = (((0, 32), (32, 32), (64, 32), (96, 16)), ((0, 32), (32, 32), (64, 32), (96, 32)), ((0, 512), (512, 512)))
WHOLE = (112, 128, 1024)

PROJECT, ATTEND, UPDATE, RENEW = range(4)
ORDER = "Q000 Q001 T000 T001 Q010 O000 O001 Q011 R000 T010 R001 T011 Q100 O010 Q101 O011".split()
ORDER += "R010 T100 R011 Q110 O100 Q111 T101 T110 T111 O101 O110 O111 R100 R101 R110 R111".split()
CODES = [8 * "QTOR".index(e[0]) + int(e[1:], 2) for e in ORDER]
WORDS = [sum(code << (5 * n) for n, code in enumerate(CODES[i : i + 4])) for i in range(0, 32, 4)]


def remote(src, dst, send_sem, recv_sem, device):
    return pltpu.make_async_remote_copy(
        src_ref=src,
        dst_ref=dst,
        send_sem=send_sem,
        recv_sem=recv_sem,
        device_id=device,
        device_id_type=MESH,
    )


def kernel(
    text, patches, tokens, conn, wq, wkv, wo, cosine, sine, out,
    CN, WQ, WO, PNS, PN, TS, T0, IS, IR, H, QS, QR, KS, VS, AR, OS, OR, FS, FR,
    own_s, own_r, z_s, z_r, f_s, f_r, p_s, p_r, t_s, t_r, i_s, i_r,
    h_s, h_r, q_s, q_r, a_s, a_r, o_s, o_r, e_s, e_r,
):
    c = lax.axis_index("pipe")
    d = lax.axis_index("dp")
    y = lax.axis_index("tensor")
    z = lax.div(d, NX)
    x = lax.rem(d, NX)

    def at(core, zz, xx, yy):
        return (core, zz * NX + xx, yy)

    def xk(k):
        return lax.rem(x + k, NX)

    def yk(k):
        return lax.rem(y + k, NY)

    def zk(k):
        return lax.rem(z + k + NZ, NZ)

    barrier = pltpu.get_barrier_semaphore()
    greeted = [at(1 - c, z, xk(k), y) for k in range(4)]
    greeted += [at(c, z, xk(k), y) for k in range(1, 4)]
    greeted += [at(c, z, x, yk(k)) for k in range(1, 4)]
    greeted += [at(c, zk(1), x, y), at(c, zk(-1), x, y)]
    for device in greeted:
        pl.semaphore_signal(barrier, inc=1, device_id=device, device_id_type=MESH)
    pl.semaphore_wait(barrier, len(greeted))

    zrow = pl.multiple_of(z * 128, 128)
    WQ[c, pl.ds(zrow, 128), pl.ds(0, 1024)] = wq[0]
    WQ[c, pl.ds(zrow, 128), pl.ds(1024, 256)] = wkv[0, 0]
    WQ[c, pl.ds(zrow, 128), pl.ds(1280, 256)] = wkv[0, 1]
    WO[c, :, pl.ds(zrow, 128)] = wo[0]
    CN[z, pl.ds(0, 96)] = conn[pl.ds(0, 96)]
    CN[z, pl.ds(96, 16)] = jnp.zeros((16, 1024), BF)
    CN[z, pl.ds(96, 4)] = conn[pl.ds(96, 4)]

    def kind(item):
        return 0 if item == 0 else 2 - item % 2

    def rows_of(item, zz, start, size):
        s = (item - 1) // 2
        if item == 0:
            return CN.at[zz, pl.ds(start, size)]
        if item % 2 == 1:
            return WQ.at[s, pl.ds(pl.multiple_of(zz * 128 + start, 32), size)]
        return WO.at[s, pl.ds(start, size), pl.ds(pl.multiple_of(zz * 128, 128), 128)]

    def block(item, zz):
        return rows_of(item, zz, 0, WHOLE[kind(item)])

    def own_copy(s, n):
        ref = block(1 + 2 * s + n, z)
        return remote(ref, ref, own_s.at[n], own_r.at[n], at(1 - s, z, x, y))

    def piece_ways(item, step):
        count = len(PIECES[kind(item)])
        return [(p, w) for p in range(count) for w in range(2) if step < 4 or p // (count // 2) == w]

    def piece_copy(item, step, piece, way, arriving):
        hops = step if arriving else step - 1
        zz = zk(-hops) if way == 0 else zk(hops)
        ref = rows_of(item, zz, *PIECES[kind(item)][piece])
        target = at(1, zk(1) if way == 0 else zk(-1), x, y)
        index = (item, step - 1, way, piece)
        return remote(ref, ref, z_s.at[index], z_r.at[index], target)

    def hand_over(item, index):
        step = index // 2 + 1
        zz = zk(-step) if index % 2 == 0 else zk(step)
        ref = block(item, zz)
        return remote(ref, ref, f_s.at[item, index], f_r.at[item, index], at(0, z, x, y))

    def patch_copy(k):
        return remote(PNS.at[xk(k)], PN.at[x, :, c], p_s.at[k], p_r.at[x, c], at(0, z, xk(k), y))

    def patch_arrival(source, core):
        ref = PN.at[source, :, core]
        return remote(ref, ref, p_s.at[0], p_r.at[source, core], at(0, z, x, y))

    def normed_patches():
        values = patches[...].reshape(64, 3200).astype(F32)
        centered = values - jnp.sum(values, axis=-1, keepdims=True) / 3200.0
        variance = jnp.sum(centered * centered, axis=-1, keepdims=True) / 3200.0
        normed = centered * lax.rsqrt(variance + 1e-06)
        row = lax.broadcasted_iota(jnp.int32, (64, 1), 0)
        limit = jnp.where(row < 32, tokens[0], tokens[1])
        normed = jnp.where(c * 32 + lax.rem(row, 32) < limit, normed, 0.0)
        lane = lax.broadcasted_iota(jnp.int32, (64, 128), 1)
        for j in range(32):
            zz, xx = divmod(j, NX)
            base = (100 * j) // 128 * 128
            offset = 100 * j - base
            width = 128 if offset + 100 <= 128 else 256
            window = normed[:, base : base + width]
            if offset:
                window = pltpu.roll(window, width - offset, 1)
            part = jnp.where(lane < 100, window[:, :128], 0.0)
            PNS[xx, :, :, zz * 128 : (zz + 1) * 128] = part.astype(BF).reshape(2, 32, 128)

    @pl.when(c == 1)
    def _():
        own = [own_copy(1, 0), own_copy(1, 1)]
        for copy in own:
            copy.start()
        for piece, way in piece_ways(0, 1):
            piece_copy(0, 1, piece, way, False).start()
        normed_patches()
        for k in range(4):
            patch_copy(k).start()
        for item, step in RING:
            onward = piece_ways(item, step) if step < 5 else []
            if step == 1:
                if item in (1, 2):
                    own_copy(0, item - 1).wait_recv()
                for piece, way in onward:
                    piece_copy(item, 1, piece, way, False).start()
            else:
                for piece, way in piece_ways(item, step - 1):
                    piece_copy(item, step - 1, piece, way, True).wait_recv()
                    if (piece, way) in onward:
                        piece_copy(item, step, piece, way, False).start()
                for index in (6,) if step == 5 else (2 * step - 4, 2 * step - 3):
                    hand_over(item, index).start()
        for copy in own:
            copy.wait_send()
        for k in range(4):
            patch_copy(k).wait_send()
        for item in range(5):
            for step in range(1, 5):
                for piece, way in piece_ways(item, step):
                    piece_copy(item, step, piece, way, False).wait_send()
            for index in range(7):
                hand_over(item, index).wait_send()

    def wait_item(item):
        for index in range(7):
            hand_over(item, index).wait_recv()

    def text_copy(half, k):
        target = at(0, z, xk(k), y)
        if half == 1:
            return remote(TS.at[xk(k), :, 1], H.at[0, :, 1, y, x], t_s.at[1, k], t_r.at[1, x], target)
        return remote(TS.at[xk(k), :, 0], T0.at[:, x], t_s.at[0, k], t_r.at[0, x], target)

    def text_arrival(half, k):
        ref = H.at[0, :, 1, y, xk(k)] if half == 1 else T0.at[:, xk(k)]
        return remote(ref, ref, t_s.at[half, k], t_r.at[half, xk(k)], at(1, z, x, y))

    def image_copy(b, k):
        return remote(IS.at[b, xk(k)], IR.at[b, x], i_s.at[b, k], i_r.at[b, x], at(0, z, xk(k), y))

    def image_arrival(b, k):
        ref = IR.at[b, xk(k)]
        return remote(ref, ref, i_s.at[b, k], i_r.at[b, xk(k)], at(1, z, x, y))

    def hidden_copy(s, b, h, k):
        ref = H.at[s, b, h, y]
        return remote(ref, ref, h_s.at[s, b, h, k], h_r.at[s, b, h, y], at(0, z, x, yk(k)))

    def hidden_arrival(s, b, h, k):
        ref = H.at[s, b, h, yk(k)]
        return remote(ref, ref, h_s.at[s, b, h, k], h_r.at[s, b, h, yk(k)], at(1, z, x, y))

    def qkv_copy(s, b, h, k):
        return remote(
            QS.at[s, b, h, xk(k)], QR.at[s, b, h, x], q_s.at[s, b, h, k], q_r.at[s, b, h, x], at(0, z, xk(k), y)
        )

    def qkv_arrival(s, b, h, k):
        ref = QR.at[s, b, h, xk(k)]
        return remote(ref, ref, q_s.at[s, b, h, k], q_r.at[s, b, h, xk(k)], at(1, z, x, y))

    def attended_copy(s, b, h, k):
        ref = AR.at[s, b, h, x]
        return remote(ref, ref, a_s.at[s, b, h, k], a_r.at[s, b, h, x], at(0, z, xk(k), y))

    def attended_arrival(s, b, h, k):
        ref = AR.at[s, b, h, xk(k)]
        return remote(ref, ref, a_s.at[s, b, h, k], a_r.at[s, b, h, xk(k)], at(1, z, x, y))

    def update_copy(s, b, h, k):
        return remote(
            OS.at[s, b, h, yk(k)], OR.at[s, b, h, y], o_s.at[s, b, h, k], o_r.at[s, b, h, y], at(0, z, x, yk(k))
        )

    def update_arrival(s, b, h, k):
        ref = OR.at[s, b, h, yk(k)]
        return remote(ref, ref, o_s.at[s, b, h, k], o_r.at[s, b, h, yk(k)], at(1, z, x, y))

    def final_copy(b, h, k):
        return remote(FS.at[b, h, xk(k)], FR.at[x, b], e_s.at[b, h, k], e_r.at[x, b], at(h, z, xk(k), y))

    def final_arrival(b, k):
        ref = FR.at[xk(k), b]
        return remote(ref, ref, e_s.at[b, 0, k], e_r.at[xk(k), b], at(1 - c, z, x, y))

    def send_text():
        position = lax.broadcasted_iota(jnp.int32, (128, 1), 0)
        for b in range(2):
            masked = jnp.where(position < tokens[b], jnp.zeros_like(text[b]), text[b])
            for xx in range(NX):
                for zz in range(2):
                    lanes = zz * 512 + xx * 128
                    TS[xx, b, :, :, zz * 128 : (zz + 1) * 128] = masked[:, lanes : lanes + 128].reshape(2, 64, 128)
        for b in range(2):
            H[0, b, 1, y, x] = TS[x, b, 1]
            T0[b, x] = TS[x, b, 0]
        for half in (1, 0):
            for k in range(1, 4):
                text_copy(half, k).start()

    def image_part():
        for core in range(2):
            for k in range(1 - core, 4):
                patch_arrival(xk(k), core).wait_recv()
        wait_item(0)
        for b in range(2):
            rows = PN[:, b].reshape(256, 1024)
            for zz in range(2):
                for pair in range(2):
                    lanes = zz * 512 + pair * 256
                    product = jnp.dot(
                        rows, CN[:, :, lanes : lanes + 256].reshape(1024, 256), preferred_element_type=F32
                    ).astype(BF)
                    for n in range(2):
                        part = product[:, n * 128 : (n + 1) * 128]
                        IS[b, 2 * pair + n, :, :, zz * 128 : (zz + 1) * 128] = part.reshape(4, 64, 128)
            for k in range(1, 4):
                image_copy(b, k).start()
        for k in range(1, 4):
            text_arrival(0, k).wait_recv()
        for b in range(2):
            for k in range(1, 4):
                image_arrival(b, k).wait_recv()
            total = IS[b, x].astype(F32)
            for k in range(1, 4):
                total = total + IR[b, xk(k)].astype(F32)
            H[0, b, 0, y] = (total.astype(BF).astype(F32) + T0[b].astype(F32)).astype(BF)
            for k in range(1, 4):
                hidden_copy(0, b, 0, k).start()

    def project(s, b, h):
        squares = jnp.zeros((256, 256), F32)
        for q in range(4):
            values = H[s, b, h, q].reshape(256, 256).astype(F32)
            squares = squares + values * values
        squares = jnp.sum(squares, axis=-1, keepdims=True)
        high = squares.astype(BF).astype(F32)
        lane = lax.broadcasted_iota(jnp.int32, (256, 128), 1)
        QS[s, b, h, :, :, 1536:1664] = (
            jnp.where(lane < 64, high, squares - high).astype(BF).reshape(4, 64, 128)
        )

        def tile(n, _):
            lanes = pl.ds(pl.multiple_of(n * 256, 256), 256)
            total = jnp.zeros((256, 256), F32)
            for q in range(4):
                total = total + jnp.dot(
                    H[s, b, h, q].reshape(256, 256),
                    WQ[s, pl.ds(q * 256, 256), lanes],
                    preferred_element_type=F32,
                )
            QS[s, b, h, :, :, lanes] = total.astype(BF).reshape(4, 64, 256)
            return 0

        lax.fori_loop(0, 6, tile, 0)
        for k in range(1, 4):
            qkv_copy(s, b, h, k).start()

    def attend(s, b, h):
        for k in range(1, 4):
            qkv_arrival(s, b, h, k).wait_recv()

        def summed(start):
            lanes = slice(start, start + 128)
            total = QS[s, b, h, x, :, lanes].astype(F32)
            for k in range(1, 4):
                total = total + QR[s, b, h, xk(k), :, lanes].astype(F32)
            return total

        squares = summed(1536)
        scale = lax.rsqrt((squares[:, 0:1] + squares[:, 64:65]) / 4096.0 + 1e-05)
        half = pl.ds(pl.multiple_of(h * 64, 64), 64)
        cos_rows = cosine[half]
        sin_rows = sine[half]

        def rotated(start):
            rows = summed(start) * scale
            return (rows * cos_rows + pltpu.roll(rows, 64, 1) * sin_rows).astype(BF)

        row = lax.rem(lax.broadcasted_iota(jnp.int32, (256, 128), 0), 64) + h * 64
        column = lax.broadcasted_iota(jnp.int32, (256, 128), 1)
        for g in range(2):
            KS[b, g, half] = rotated(1024 + g * 128)
            VS[b, g, half] = (summed(1280 + g * 128) * scale).astype(BF)
            stacked = jnp.concatenate([rotated((4 * g + j) * 128) for j in range(4)], axis=0)
            scores = lax.dot_general(
                stacked, KS[b, g], (((1,), (1,)), ((), ())), preferred_element_type=F32
            )
            scores = jnp.where(row >= column, scores * SCALE, -1e30)
            weights = jnp.exp(scores - jnp.max(scores, axis=-1, keepdims=True))
            norm = jnp.sum(weights, axis=-1, keepdims=True)
            mixed = jnp.dot(weights.astype(BF), VS[b, g], preferred_element_type=F32) / norm
            for j in range(4):
                lanes = (4 * g + j) * 128
                AR[s, b, h, x, :, lanes : lanes + 128] = mixed[j * 64 : (j + 1) * 64].astype(BF)
        for k in range(1, 4):
            attended_copy(s, b, h, k).start()

    def update(s, b, h):
        for k in range(1, 4):
            attended_arrival(s, b, h, k).wait_recv()

        def tile(n, _):
            yd = yk(n + 1)
            lanes = pl.ds(pl.multiple_of(yd * 256, 256), 256)
            product = jnp.dot(AR[s, b, h].reshape(256, 1024), WO[s, :, lanes], preferred_element_type=F32)
            OS[s, b, h, yd] = product.astype(BF).reshape(4, 64, 256)

            @pl.when(n < 3)
            def _():
                update_copy(s, b, h, n + 1).start()

            return 0

        lax.fori_loop(0, 4, tile, 0)

    def renew(s, b, h):
        for k in range(1, 4):
            update_arrival(s, b, h, k).wait_recv()
        total = OS[s, b, h, y].astype(F32)
        for k in range(1, 4):
            total = total + OR[s, b, h, yk(k)].astype(F32)
        fresh = (H[s, b, h, y].astype(F32) + total).astype(BF)

        @pl.when(s == 0)
        def _():
            H[1, b, h, y] = fresh
            for k in range(1, 4):
                hidden_copy(1, b, h, k).start()

        @pl.when(s == 1)
        def _():
            FS[b, h] = fresh
            for k in range(1, 4):
                final_copy(b, h, k).start()

            @pl.when(h == 0)
            def _():
                FR[x, b] = FS[b, 0, x]

            @pl.when(h == 1)
            def _():
                final_copy(b, h, 0).start()

    @pl.when(c == 0)
    def _():
        own_copy(0, 0).start()
        own_copy(0, 1).start()
        send_text()
        for zz in range(NZ):
            CN[zz, pl.ds(112, 16)] = jnp.zeros((16, 1024), BF)
        KS[...] = jnp.zeros_like(KS)
        VS[...] = jnp.zeros_like(VS)
        normed_patches()
        PN[x, :, 0] = PNS[x]
        for k in range(1, 4):
            patch_copy(k).start()
        for k in range(1, 4):
            text_arrival(1, k).wait_recv()
        for b in range(2):
            for k in range(1, 4):
                hidden_copy(0, b, 1, k).start()
        image_part()

        def stage(n, word):
            fresh = jnp.int32(WORDS[7])
            for m in range(7):
                fresh = jnp.where(lax.div(n, 4) == m, jnp.int32(WORDS[m]), fresh)
            word = jnp.where(lax.rem(n, 4) == 0, fresh, word)
            code = lax.rem(word, 32)
            what = lax.div(code, 8)
            s = lax.rem(lax.div(code, 4), 2)
            b = lax.rem(lax.div(code, 2), 2)
            h = lax.rem(code, 2)
            first = lax.rem(code, 4) == 0

            @pl.when(what == PROJECT)
            def _():
                @pl.when(first & (s == 0))
                def _():
                    wait_item(1)

                @pl.when(first & (s == 1))
                def _():
                    own_copy(1, 0).wait_recv()
                    wait_item(3)

                for k in range(1, 4):
                    hidden_arrival(s, b, h, k).wait_recv()
                project(s, b, h)

            @pl.when(what == ATTEND)
            def _():
                attend(s, b, h)

            @pl.when(what == UPDATE)
            def _():
                @pl.when(first & (s == 0))
                def _():
                    wait_item(2)

                @pl.when(first & (s == 1))
                def _():
                    own_copy(1, 1).wait_recv()
                    wait_item(4)

                update(s, b, h)

            @pl.when(what == RENEW)
            def _():
                renew(s, b, h)

            return lax.div(word, 32)

        lax.fori_loop(0, 32, stage, jnp.int32(0))

    for b in range(2):

        @pl.when(c == 1)
        def _():
            final_arrival(b, 0).wait_recv()

        for k in range(1, 4):
            final_arrival(b, k).wait_recv()
    for b in range(2):
        for xx in range(NX):
            for zz in range(2):
                lanes = zz * 512 + xx * 128
                out[b, :, lanes : lanes + 128] = FR[xx, b, :, zz * 128 : (zz + 1) * 128]

    @pl.when(c == 0)
    def _():
        own_copy(0, 0).wait_send()
        own_copy(0, 1).wait_send()
        for k in range(1, 4):
            patch_copy(k).wait_send()
            text_copy(0, k).wait_send()
            text_copy(1, k).wait_send()
            image_copy(0, k).wait_send()
            image_copy(1, k).wait_send()

        def drain(n, _):
            s, b = lax.div(n, 2), lax.rem(n, 2)
            for k in range(1, 4):
                for h in range(2):
                    hidden_copy(s, b, h, k).wait_send()
                    qkv_copy(s, b, h, k).wait_send()
                    attended_copy(s, b, h, k).wait_send()
                    update_copy(s, b, h, k).wait_send()
            return 0

        lax.fori_loop(0, 4, drain, 0)
        for b in range(2):
            for h in range(2):
                for k in range(1 - h, 4):
                    final_copy(b, h, k).wait_send()


def rotation_tables():
    frequencies = 500000.0 ** (-(np.arange(64, dtype=np.float32) * np.float32(2.0) / np.float32(128)))
    angles = np.arange(128, dtype=np.float32)[:, None] * frequencies.astype(np.float32)[None, :]
    cosine, sine = np.cos(angles), np.sin(angles)
    return (
        np.concatenate([cosine, cosine], axis=1).astype(np.float32),
        np.concatenate([-sine, sine], axis=1).astype(np.float32),
    )


def shards(text_embeds, patches, image_tokens, connector, w_query, w_keyval, w_out):
    cosine, sine = rotation_tables()
    vmem = pl.BlockSpec(memory_space=pltpu.VMEM)
    dma = pltpu.SemaphoreType.DMA
    return pl.pallas_call(
        kernel,
        out_shape=jax.ShapeDtypeStruct((2, 64, 1024), BF),
        in_specs=[vmem, vmem, pl.BlockSpec(memory_space=pltpu.SMEM)] + [vmem] * 6,
        out_specs=vmem,
        scratch_shapes=[
            pltpu.VMEM((8, 128, 1024), BF),
            pltpu.VMEM((2, 1024, 1536), BF),
            pltpu.VMEM((2, 1024, 1024), BF),
            pltpu.VMEM((4, 2, 32, 1024), BF),
            pltpu.VMEM((4, 2, 2, 32, 1024), BF),
            pltpu.VMEM((4, 2, 2, 64, 256), BF),
            pltpu.VMEM((2, 4, 64, 256), BF),
            pltpu.VMEM((2, 4, 4, 64, 256), BF),
            pltpu.VMEM((2, 4, 4, 64, 256), BF),
            pltpu.VMEM((2, 2, 2, 4, 4, 64, 256), BF),
            pltpu.VMEM((2, 2, 2, 4, 64, 1664), BF),
            pltpu.VMEM((2, 2, 2, 4, 64, 1664), BF),
            pltpu.VMEM((2, 2, 128, 128), BF),
            pltpu.VMEM((2, 2, 128, 128), BF),
            pltpu.VMEM((2, 2, 2, 4, 64, 1024), BF),
            pltpu.VMEM((2, 2, 2, 4, 4, 64, 256), BF),
            pltpu.VMEM((2, 2, 2, 4, 4, 64, 256), BF),
            pltpu.VMEM((2, 2, 4, 64, 256), BF),
            pltpu.VMEM((4, 2, 64, 256), BF),
            dma((2,)), dma((2,)),
            dma((5, 4, 2, 4)), dma((5, 4, 2, 4)),
            dma((5, 7)), dma((5, 7)),
            dma((4,)), dma((4, 2)),
            dma((2, 4)), dma((2, 4)),
            dma((2, 4)), dma((2, 4)),
            dma((2, 2, 2, 4)), dma((2, 2, 2, 4)),
            dma((2, 2, 2, 4)), dma((2, 2, 2, 4)),
            dma((2, 2, 2, 4)), dma((2, 2, 2, 4)),
            dma((2, 2, 2, 4)), dma((2, 2, 2, 4)),
            dma((2, 2, 4)), dma((4, 2)),
        ],
        compiler_params=pltpu.CompilerParams(
            collective_id=0, has_side_effects=True, vmem_limit_bytes=62 * 2**20
        ),
        cost_estimate=pl.CostEstimate(flops=11 * 10**9, bytes_accessed=20 * 10**6, transcendentals=10**6),
        name="decoder",
    )(text_embeds, patches, image_tokens, connector, w_query, w_keyval, w_out, cosine, sine)


def solution(mesh):
    placed = (
        P("dp", None, "tensor"),
        P("dp", "pipe", None),
        P("dp"),
        P("dp", "tensor"),
        P("pipe", "dp", "tensor"),
        P("pipe", None, "dp", "tensor"),
        P("pipe", "tensor", "dp"),
    )
    return jax.shard_map(
        shards, mesh=mesh, in_specs=placed, out_specs=P("dp", "pipe", "tensor"), check_vma=False
    )
```

```python
import math

import jax
import jax.numpy as jnp
import numpy as np
from jax import lax
from jax.experimental import pallas as pl
from jax.experimental.pallas import tpu as pltpu
from jax.sharding import PartitionSpec as P

MESH = pl.DeviceIdType.MESH
BF = jnp.bfloat16
F32 = jnp.float32
NX, NY, NZ = 4, 4, 8
SCALE = 1.0 / math.sqrt(128)

RING = [
    (0, 2), (0, 3), (0, 4), (1, 2), (1, 3), (2, 1), (1, 4), (2, 2), (2, 3), (3, 1), (2, 4),
    (3, 2), (3, 3), (4, 1), (3, 4), (4, 2), (4, 3), (4, 4),
]
PIECES = (((0, 32), (32, 32), (64, 32), (96, 16)), ((0, 32), (32, 32), (64, 32), (96, 32)), ((0, 512), (512, 512)))
WHOLE = (112, 128, 1024)

PROJECT, ATTEND, UPDATE, RENEW = range(4)
CODES = (
    1, 0, 2, 8, 9, 3, 16, 10, 17, 24, 11, 25, 18, 4, 19, 5, 26, 27, 12, 6, 13, 20, 7, 21, 14, 15, 22, 23, 28, 29, 30, 31,
)
AWAITED = {8 * PROJECT: 1, 8 * PROJECT + 4: 3, 8 * UPDATE: 2, 8 * UPDATE + 4: 4}
FIRST = {item: min(n for n, code in enumerate(CODES) if code // 4 == at // 4) for at, item in AWAITED.items()}
WORDS = [sum(code << (5 * n) for n, code in enumerate(CODES[i : i + 4])) for i in range(0, 32, 4)]


def remote(src, dst, send_sem, recv_sem, device):
    return pltpu.make_async_remote_copy(
        src_ref=src,
        dst_ref=dst,
        send_sem=send_sem,
        recv_sem=recv_sem,
        device_id=device,
        device_id_type=MESH,
    )


def kernel(
    text, patches, tokens, conn, wq, wkv, wo, cosine, sine, out,
    CN, WQ, WO, PNS, PN, TS, T0, IS, IR, H, QS, QR, KS, VS, AR, OS, OR, FS, FR,
    own_s, own_r, z_s, z_r, f_s, f_r, p_s, p_r, t_s, t_r, i_s, i_r,
    h_s, h_r, q_s, q_r, a_s, a_r, o_s, o_r, e_s, e_r,
):
    c = lax.axis_index("pipe")
    d = lax.axis_index("dp")
    y = lax.axis_index("tensor")
    z = lax.div(d, NX)
    x = lax.rem(d, NX)

    def at(core, zz, xx, yy):
        return (core, zz * NX + xx, yy)

    def xk(k):
        return lax.rem(x + k, NX)

    def yk(k):
        return lax.rem(y + k, NY)

    def zk(k):
        return lax.rem(z + k + NZ, NZ)

    barrier = pltpu.get_barrier_semaphore()
    greeted = [at(1 - c, z, xk(k), y) for k in range(4)]
    greeted += [at(c, z, xk(k), y) for k in range(1, 4)]
    greeted += [at(c, z, x, yk(k)) for k in range(1, 4)]
    greeted += [at(core, zk(way), x, y) for core in range(2) for way in (1, -1)]
    for device in greeted:
        pl.semaphore_signal(barrier, inc=1, device_id=device, device_id_type=MESH)
    pl.semaphore_wait(barrier, len(greeted))

    zrow = pl.multiple_of(z * 128, 128)
    WQ[c, pl.ds(zrow, 128), pl.ds(0, 1024)] = wq[0]
    WQ[c, pl.ds(zrow, 128), pl.ds(1024, 256)] = wkv[0, 0]
    WQ[c, pl.ds(zrow, 128), pl.ds(1280, 256)] = wkv[0, 1]
    WO[c, :, pl.ds(zrow, 128)] = wo[0]
    CN[z, pl.ds(0, 96)] = conn[pl.ds(0, 96)]
    CN[z, pl.ds(96, 16)] = jnp.zeros((16, 1024), BF)
    CN[z, pl.ds(96, 4)] = conn[pl.ds(96, 4)]

    def kind(item):
        return 0 if item == 0 else 2 - item % 2

    def rows_of(item, zz, start, size):
        s = (item - 1) // 2
        if item == 0:
            return CN.at[zz, pl.ds(start, size)]
        if item % 2 == 1:
            return WQ.at[s, pl.ds(pl.multiple_of(zz * 128 + start, 32), size)]
        return WO.at[s, pl.ds(start, size), pl.ds(pl.multiple_of(zz * 128, 128), 128)]

    def block(item, zz):
        return rows_of(item, zz, 0, WHOLE[kind(item)])

    def own_copy(s, n):
        ref = block(1 + 2 * s + n, z)
        return remote(ref, ref, own_s.at[n], own_r.at[n], at(1 - s, z, x, y))

    def piece_ways(item, step):
        count = len(PIECES[kind(item)])
        return [(p, w) for p in range(count) for w in range(2) if step < 4 or p // (count // 2) == w]

    def piece_copy(item, step, piece, way, arriving):
        hops = step if arriving else step - 1
        zz = zk(-hops) if way == 0 else zk(hops)
        ref = rows_of(item, zz, *PIECES[kind(item)][piece])
        target = at(1 if step < 4 else 0, zk(1) if way == 0 else zk(-1), x, y)
        arrived = z_r.at[item % 3, step - 1, way, piece] if step < 4 else f_r.at[item]
        return remote(ref, ref, z_s.at[item], arrived, target)

    def blocks(item, count):
        s = (item - 1) // 2
        if item == 0:
            return CN.at[pl.ds(0, count), pl.ds(0, 112)]
        if item % 2 == 1:
            return WQ.at[s, pl.ds(0, 128 * count)]
        return WO.at[s, :, pl.ds(0, 128 * count)]

    def waits(ref, semaphore):
        return remote(ref, ref, semaphore, semaphore, at(1 - c, z, x, y))

    def hand_over(item, index):
        step = index // 2 + 1
        zz = zk(-step) if index % 2 == 0 else zk(step)
        ref = block(item, zz)
        return remote(ref, ref, f_s.at[item], f_r.at[item], at(0, z, x, y))

    def patch_copy(k):
        return remote(PNS.at[xk(k)], PN.at[x, :, c], p_s.at[0], p_r.at[c], at(0, z, xk(k), y))

    def normed_patches():
        values = patches[...].reshape(64, 3200).astype(F32)
        centered = values - jnp.sum(values, axis=-1, keepdims=True) / 3200.0
        variance = jnp.sum(centered * centered, axis=-1, keepdims=True) / 3200.0
        normed = centered * lax.rsqrt(variance + 1e-06)
        row = lax.broadcasted_iota(jnp.int32, (64, 1), 0)
        limit = jnp.where(row < 32, tokens[0], tokens[1])
        normed = jnp.where(c * 32 + lax.rem(row, 32) < limit, normed, 0.0)
        lane = lax.broadcasted_iota(jnp.int32, (64, 128), 1)
        for j in range(32):
            zz, xx = divmod(j, NX)
            base = (100 * j) // 128 * 128
            offset = 100 * j - base
            width = 128 if offset + 100 <= 128 else 256
            window = normed[:, base : base + width]
            if offset:
                window = pltpu.roll(window, width - offset, 1)
            part = jnp.where(lane < 100, window[:, :128], 0.0)
            PNS[xx, :, :, zz * 128 : (zz + 1) * 128] = part.astype(BF).reshape(2, 32, 128)

    @pl.when(c == 1)
    def _():
        own = [own_copy(1, 0), own_copy(1, 1)]
        for copy in own:
            copy.start()
        for piece, way in piece_ways(0, 1):
            piece_copy(0, 1, piece, way, False).start()
        normed_patches()
        for k in range(4):
            patch_copy(k).start()
        own_copy(0, 0).wait_recv()
        for way in range(2):
            piece_copy(1, 1, 0, way, False).start()
        for item, step in RING:
            if step == 1:
                if item == 2:
                    own_copy(0, 1).wait_recv()
                for piece, way in piece_ways(item, 1):
                    piece_copy(item, 1, piece, way, False).start()
            else:
                onward = piece_ways(item, step)
                for piece, way in piece_ways(item, step - 1):
                    piece_copy(item, step - 1, piece, way, True).wait_recv()
                    if (piece, way) in onward:
                        piece_copy(item, step, piece, way, False).start()
                if item == 0:
                    for way in range(2):
                        piece_copy(1, 1, step - 1, way, False).start()
                for index in (2 * step - 4, 2 * step - 3):
                    hand_over(item, index).start()
        for copy in own:
            copy.wait_send()
        waits(PNS, p_s.at[0]).wait_send()
        for item in range(5):
            waits(blocks(item, 7), z_s.at[item]).wait_send()
            waits(blocks(item, 6), f_s.at[item]).wait_send()

    def wait_item(item):
        waits(blocks(item, 7), f_r.at[item]).wait_recv()

    def text_copy(half, k):
        target = at(0, z, xk(k), y)
        if half == 1:
            return remote(TS.at[xk(k), :, 1], H.at[0, :, 1, y, x], t_s.at[0], t_r.at[1], target)
        return remote(TS.at[xk(k), :, 0], T0.at[:, x], t_s.at[0], t_r.at[0], target)

    def text_arrival(half):
        waits(H.at[0, :, 1, y, pl.ds(0, 3)] if half == 1 else T0.at[:, pl.ds(0, 3)], t_r.at[half]).wait_recv()

    def image_copy(b, k):
        return remote(IS.at[b, xk(k)], IR.at[b, x], i_s.at[0], i_r.at[b], at(0, z, xk(k), y))

    def image_arrival(b):
        waits(IR.at[b, pl.ds(0, 3)], i_r.at[b]).wait_recv()

    def hidden_copy(s, b, h, k):
        ref = H.at[s, b, h, y]
        return remote(ref, ref, h_s.at[0], h_r.at[b, h], at(0, z, x, yk(k)))

    def hidden_arrival(s, b, h):
        waits(H.at[s, b, h, pl.ds(0, 3)], h_r.at[b, h]).wait_recv()

    def qkv_copy(s, b, h, k):
        return remote(QS.at[s, b, h, xk(k)], QR.at[s, b, h, x], q_s.at[0], q_r.at[b, h], at(0, z, xk(k), y))

    def qkv_arrival(s, b, h):
        waits(QR.at[s, b, h, pl.ds(0, 3)], q_r.at[b, h]).wait_recv()

    def attended_copy(s, b, h, k):
        ref = AR.at[s, b, h, x]
        return remote(ref, ref, a_s.at[0], a_r.at[b, h], at(0, z, xk(k), y))

    def attended_arrival(s, b, h):
        waits(AR.at[s, b, h, pl.ds(0, 3)], a_r.at[b, h]).wait_recv()

    def update_copy(s, b, h, k):
        return remote(OS.at[s, b, h, yk(k)], OR.at[s, b, h, y], o_s.at[0], o_r.at[b, h], at(0, z, x, yk(k)))

    def update_arrival(s, b, h):
        waits(OR.at[s, b, h, pl.ds(0, 3)], o_r.at[b, h]).wait_recv()

    def final_copy(b, h, k):
        return remote(FS.at[b, h, xk(k)], FR.at[x, b], e_s.at[h], e_r.at[b], at(h, z, xk(k), y))

    def send_text():
        position = lax.broadcasted_iota(jnp.int32, (128, 1), 0)
        for b in range(2):
            masked = jnp.where(position < tokens[b], jnp.zeros_like(text[b]), text[b])
            for xx in range(NX):
                for zz in range(2):
                    lanes = zz * 512 + xx * 128
                    TS[xx, b, :, :, zz * 128 : (zz + 1) * 128] = masked[:, lanes : lanes + 128].reshape(2, 64, 128)
        for b in range(2):
            H[0, b, 1, y, x] = TS[x, b, 1]
            T0[b, x] = TS[x, b, 0]
        for half in (1, 0):
            for k in range(1, 4):
                text_copy(half, k).start()

    def image_part():
        waits(PN.at[pl.ds(0, 3), :, 0], p_r.at[0]).wait_recv()
        waits(PN.at[:, :, 1], p_r.at[1]).wait_recv()
        wait_item(0)
        for b in range(2):
            rows = PN[:, b].reshape(256, 1024)
            for zz in range(2):
                for pair in range(2):
                    lanes = zz * 512 + pair * 256
                    product = jnp.dot(
                        rows, CN[:, :, lanes : lanes + 256].reshape(1024, 256), preferred_element_type=F32
                    ).astype(BF)
                    for n in range(2):
                        part = product[:, n * 128 : (n + 1) * 128]
                        IS[b, 2 * pair + n, :, :, zz * 128 : (zz + 1) * 128] = part.reshape(4, 64, 128)
            for k in range(1, 4):
                image_copy(b, k).start()
        text_arrival(0)
        for b in range(2):
            image_arrival(b)
            total = IS[b, x].astype(F32)
            for k in range(1, 4):
                total = total + IR[b, xk(k)].astype(F32)
            H[0, b, 0, y] = (total.astype(BF).astype(F32) + T0[b].astype(F32)).astype(BF)
            for k in range(1, 4):
                hidden_copy(0, b, 0, k).start()

    def project(s, b, h):
        squares = jnp.zeros((256, 256), F32)
        for q in range(4):
            values = H[s, b, h, q].reshape(256, 256).astype(F32)
            squares = squares + values * values
        squares = jnp.sum(squares, axis=-1, keepdims=True)
        high = squares.astype(BF).astype(F32)
        lane = lax.broadcasted_iota(jnp.int32, (256, 128), 1)
        QS[s, b, h, :, :, 1536:1664] = (
            jnp.where(lane < 64, high, squares - high).astype(BF).reshape(4, 64, 128)
        )

        def tile(n, _):
            lanes = pl.ds(pl.multiple_of(n * 256, 256), 256)
            total = jnp.zeros((256, 256), F32)
            for q in range(4):
                total = total + jnp.dot(
                    H[s, b, h, q].reshape(256, 256),
                    WQ[s, pl.ds(q * 256, 256), lanes],
                    preferred_element_type=F32,
                )
            QS[s, b, h, :, :, lanes] = total.astype(BF).reshape(4, 64, 256)
            return 0

        lax.fori_loop(0, 6, tile, 0)
        for k in range(1, 4):
            qkv_copy(s, b, h, k).start()

    def attend(s, b, h):
        qkv_arrival(s, b, h)

        def summed(start):
            lanes = slice(start, start + 128)
            total = QS[s, b, h, x, :, lanes].astype(F32)
            for k in range(1, 4):
                total = total + QR[s, b, h, xk(k), :, lanes].astype(F32)
            return total

        squares = summed(1536)
        scale = lax.rsqrt((squares[:, 0:1] + squares[:, 64:65]) / 4096.0 + 1e-05)
        half = pl.ds(pl.multiple_of(h * 64, 64), 64)
        cos_rows = cosine[half]
        sin_rows = sine[half]

        def rotated(start):
            rows = summed(start) * scale
            return (rows * cos_rows + pltpu.roll(rows, 64, 1) * sin_rows).astype(BF)

        row = lax.rem(lax.broadcasted_iota(jnp.int32, (256, 128), 0), 64) + h * 64
        column = lax.broadcasted_iota(jnp.int32, (256, 128), 1)
        for g in range(2):
            KS[b, g, half] = rotated(1024 + g * 128)
            VS[b, g, half] = (summed(1280 + g * 128) * scale).astype(BF)
            stacked = jnp.concatenate([rotated((4 * g + j) * 128) for j in range(4)], axis=0)
            scores = lax.dot_general(
                stacked, KS[b, g], (((1,), (1,)), ((), ())), preferred_element_type=F32
            )
            scores = jnp.where(row >= column, scores * SCALE, -1e30)
            weights = jnp.exp(scores - jnp.max(scores, axis=-1, keepdims=True))
            norm = jnp.sum(weights, axis=-1, keepdims=True)
            mixed = jnp.dot(weights.astype(BF), VS[b, g], preferred_element_type=F32) / norm
            for j in range(4):
                lanes = (4 * g + j) * 128
                AR[s, b, h, x, :, lanes : lanes + 128] = mixed[j * 64 : (j + 1) * 64].astype(BF)
        for k in range(1, 4):
            attended_copy(s, b, h, k).start()

    def update(s, b, h):
        attended_arrival(s, b, h)

        def tile(n, _):
            yd = yk(n + 1)
            lanes = pl.ds(pl.multiple_of(yd * 256, 256), 256)
            product = jnp.dot(AR[s, b, h].reshape(256, 1024), WO[s, :, lanes], preferred_element_type=F32)
            OS[s, b, h, yd] = product.astype(BF).reshape(4, 64, 256)

            @pl.when(n < 3)
            def _():
                update_copy(s, b, h, n + 1).start()

            return 0

        lax.fori_loop(0, 4, tile, 0)

    def renew(s, b, h):
        update_arrival(s, b, h)
        total = OS[s, b, h, y].astype(F32)
        for k in range(1, 4):
            total = total + OR[s, b, h, yk(k)].astype(F32)
        fresh = (H[s, b, h, y].astype(F32) + total).astype(BF)

        @pl.when(s == 0)
        def _():
            H[1, b, h, y] = fresh
            for k in range(1, 4):
                hidden_copy(1, b, h, k).start()

        @pl.when(s == 1)
        def _():
            FS[b, h] = fresh
            for k in range(1, 4):
                final_copy(b, h, k).start()

            @pl.when(h == 0)
            def _():
                FR[x, b] = FS[b, 0, x]

            @pl.when(h == 1)
            def _():
                final_copy(b, h, 0).start()

    @pl.when(c == 0)
    def _():
        own_copy(0, 0).start()
        own_copy(0, 1).start()
        send_text()
        for zz in range(NZ):
            CN[zz, pl.ds(112, 16)] = jnp.zeros((16, 1024), BF)
        KS[...] = jnp.zeros_like(KS)
        VS[...] = jnp.zeros_like(VS)
        normed_patches()
        PN[x, :, 0] = PNS[x]
        for k in range(1, 4):
            patch_copy(k).start()
        text_arrival(1)
        for b in range(2):
            for k in range(1, 4):
                hidden_copy(0, b, 1, k).start()
        image_part()

        def stage(n, word):
            fresh = jnp.int32(WORDS[7])
            for m in range(7):
                fresh = jnp.where(lax.div(n, 4) == m, jnp.int32(WORDS[m]), fresh)
            word = jnp.where(lax.rem(n, 4) == 0, fresh, word)
            code = lax.rem(word, 32)
            what = lax.div(code, 8)
            s = lax.rem(lax.div(code, 4), 2)
            b = lax.rem(lax.div(code, 2), 2)
            h = lax.rem(code, 2)

            for item in range(1, 5):

                @pl.when(n == FIRST[item])
                def _():
                    if item > 2:
                        own_copy(1, item - 3).wait_recv()
                    wait_item(item)

            @pl.when(what == PROJECT)
            def _():
                hidden_arrival(s, b, h)
                project(s, b, h)

            @pl.when(what == ATTEND)
            def _():
                attend(s, b, h)

            @pl.when(what == UPDATE)
            def _():
                update(s, b, h)

            @pl.when(what == RENEW)
            def _():
                renew(s, b, h)

            return lax.div(word, 32)

        lax.fori_loop(0, 32, stage, jnp.int32(0))

    for b in range(2):

        @pl.when(c == 0)
        def _():
            waits(FR.at[pl.ds(0, 3), b], e_r.at[b]).wait_recv()

        @pl.when(c == 1)
        def _():
            waits(FR.at[:, b], e_r.at[b]).wait_recv()

    for b in range(2):
        for xx in range(NX):
            for zz in range(2):
                lanes = zz * 512 + xx * 128
                out[b, :, lanes : lanes + 128] = FR[xx, b, :, zz * 128 : (zz + 1) * 128]

    @pl.when(c == 0)
    def _():
        own_copy(0, 0).wait_send()
        own_copy(0, 1).wait_send()
        waits(PNS.at[pl.ds(0, 3)], p_s.at[0]).wait_send()
        waits(TS.at[pl.ds(0, 3)], t_s.at[0]).wait_send()
        waits(IS.at[:, pl.ds(0, 3)], i_s.at[0]).wait_send()
        for sent, semaphore in ((H, h_s), (QS, q_s), (AR, a_s), (OS, o_s)):
            waits(sent.at[:, :, :, pl.ds(0, 3)], semaphore.at[0]).wait_send()
        waits(FS.at[:, 0, pl.ds(0, 3)], e_s.at[0]).wait_send()
        waits(FS.at[:, 1], e_s.at[1]).wait_send()


def rotation_tables():
    frequencies = 500000.0 ** (-(np.arange(64, dtype=np.float32) * np.float32(2.0) / np.float32(128)))
    angles = np.arange(128, dtype=np.float32)[:, None] * frequencies.astype(np.float32)[None, :]
    cosine, sine = np.cos(angles), np.sin(angles)
    return (
        np.concatenate([cosine, cosine], axis=1).astype(np.float32),
        np.concatenate([-sine, sine], axis=1).astype(np.float32),
    )


def shards(text_embeds, patches, image_tokens, connector, w_query, w_keyval, w_out):
    cosine, sine = rotation_tables()
    vmem = pl.BlockSpec(memory_space=pltpu.VMEM)
    dma = pltpu.SemaphoreType.DMA
    return pl.pallas_call(
        kernel,
        out_shape=jax.ShapeDtypeStruct((2, 64, 1024), BF),
        in_specs=[vmem, vmem, pl.BlockSpec(memory_space=pltpu.SMEM)] + [vmem] * 6,
        out_specs=vmem,
        scratch_shapes=[
            pltpu.VMEM((8, 128, 1024), BF),
            pltpu.VMEM((2, 1024, 1536), BF),
            pltpu.VMEM((2, 1024, 1024), BF),
            pltpu.VMEM((4, 2, 32, 1024), BF),
            pltpu.VMEM((4, 2, 2, 32, 1024), BF),
            pltpu.VMEM((4, 2, 2, 64, 256), BF),
            pltpu.VMEM((2, 4, 64, 256), BF),
            pltpu.VMEM((2, 4, 4, 64, 256), BF),
            pltpu.VMEM((2, 4, 4, 64, 256), BF),
            pltpu.VMEM((2, 2, 2, 4, 4, 64, 256), BF),
            pltpu.VMEM((2, 2, 2, 4, 64, 1664), BF),
            pltpu.VMEM((2, 2, 2, 4, 64, 1664), BF),
            pltpu.VMEM((2, 2, 128, 128), BF),
            pltpu.VMEM((2, 2, 128, 128), BF),
            pltpu.VMEM((2, 2, 2, 4, 64, 1024), BF),
            pltpu.VMEM((2, 2, 2, 4, 4, 64, 256), BF),
            pltpu.VMEM((2, 2, 2, 4, 4, 64, 256), BF),
            pltpu.VMEM((2, 2, 4, 64, 256), BF),
            pltpu.VMEM((4, 2, 64, 256), BF),
            dma((2,)), dma((2,)),
            dma((5,)), dma((3, 3, 2, 4)),
            dma((5,)), dma((5,)),
            dma((1,)), dma((2,)),
            dma((1,)), dma((2,)),
            dma((1,)), dma((2,)),
            dma((1,)), dma((2, 2)),
            dma((1,)), dma((2, 2)),
            dma((1,)), dma((2, 2)),
            dma((1,)), dma((2, 2)),
            dma((2,)), dma((2,)),
        ],
        compiler_params=pltpu.CompilerParams(
            collective_id=0, has_side_effects=True, vmem_limit_bytes=62 * 2**20
        ),
        cost_estimate=pl.CostEstimate(flops=11 * 10**9, bytes_accessed=20 * 10**6, transcendentals=10**6),
        name="decoder",
    )(text_embeds, patches, image_tokens, connector, w_query, w_keyval, w_out, cosine, sine)


def solution(mesh):
    placed = (
        P("dp", None, "tensor"),
        P("dp", "pipe", None),
        P("dp"),
        P("dp", "tensor"),
        P("pipe", "dp", "tensor"),
        P("pipe", None, "dp", "tensor"),
        P("pipe", "tensor", "dp"),
    )
    return jax.shard_map(
        shards, mesh=mesh, in_specs=placed, out_specs=P("dp", "pipe", "tensor"), check_vma=False
    )
```

```python
import math

import jax
import jax.numpy as jnp
import numpy as np
from jax import lax
from jax.experimental import pallas as pl
from jax.experimental.pallas import tpu as pltpu
from jax.sharding import PartitionSpec as P

MESH = pl.DeviceIdType.MESH
BF = jnp.bfloat16
F32 = jnp.float32
NX, NY, NZ = 4, 4, 8
SCALE = 1.0 / math.sqrt(128)

RING = [
    (0, 2), (0, 3), (0, 4), (1, 2), (1, 3), (1, 4), (2, 1), (2, 2), (2, 3), (3, 1), (2, 4),
    (3, 2), (3, 3), (4, 1), (3, 4), (4, 2), (4, 3), (4, 4),
]
PIECES = (((0, 32), (32, 32), (64, 32), (96, 16)), ((0, 32), (32, 32), (64, 32), (96, 32)), ((0, 512), (512, 512)))
WHOLE = (112, 128, 1024)

PROJECT, ATTEND, UPDATE, RENEW = range(4)
CODES = (
    1, 0, 2, 8, 9, 3, 16, 10, 17, 24, 11, 25, 18, 4, 19, 5, 26, 27, 12, 6, 13, 20, 7, 21, 14, 15, 22, 23, 28, 29, 30, 31,
)
AWAITED = {8 * PROJECT: 1, 8 * PROJECT + 4: 3, 8 * UPDATE: 2, 8 * UPDATE + 4: 4}
FIRST = {item: min(n for n, code in enumerate(CODES) if code // 4 == at // 4) for at, item in AWAITED.items()}
WORDS = [sum(code << (5 * n) for n, code in enumerate(CODES[i : i + 4])) for i in range(0, 32, 4)]


def remote(src, dst, send_sem, recv_sem, device):
    return pltpu.make_async_remote_copy(
        src_ref=src,
        dst_ref=dst,
        send_sem=send_sem,
        recv_sem=recv_sem,
        device_id=device,
        device_id_type=MESH,
    )


def kernel(
    text_in, patches_in, tokens_in, conn_in, wq, wkv, wo, cosine_in, sine_in, out,
    text, patches, tokens, conn, cosine, sine,
    CN, WQ, WO, PNS, PN, TS, T0, IS, IR, H, QS, QR, KS, VS, AR, OS, OR, FS, FR,
    l_s, own_s, own_r, z_s, z_r, f_s, f_r, p_s, p_r, t_s, t_r, i_s, i_r,
    h_s, h_r, q_s, q_r, a_s, a_r, o_s, o_r, e_s, e_r,
):
    c = lax.axis_index("pipe")
    d = lax.axis_index("dp")
    y = lax.axis_index("tensor")
    z = lax.div(d, NX)
    x = lax.rem(d, NX)

    def at(core, zz, xx, yy):
        return (core, zz * NX + xx, yy)

    def xk(k):
        return lax.rem(x + k, NX)

    def yk(k):
        return lax.rem(y + k, NY)

    def zk(k):
        return lax.rem(z + k + NZ, NZ)

    zrow = pl.multiple_of(z * 128, 128)
    local = [
        (conn_in, conn),
        (wq.at[0], WQ.at[c, pl.ds(zrow, 128), pl.ds(0, 1024)]),
        (wkv.at[0, 0], WQ.at[c, pl.ds(zrow, 128), pl.ds(1024, 256)]),
        (wkv.at[0, 1], WQ.at[c, pl.ds(zrow, 128), pl.ds(1280, 256)]),
        (patches_in, patches),
        (tokens_in, tokens),
        (text_in, text),
        (wo.at[0], WO.at[c, :, pl.ds(zrow, 128)]),
        (cosine_in, cosine),
        (sine_in, sine),
    ]
    loads = [pltpu.make_async_copy(a, b, l_s.at[n]) for n, (a, b) in enumerate(local)]
    for load in loads:
        load.start()

    barrier = pltpu.get_barrier_semaphore()
    greeted = [at(1 - c, z, xk(k), y) for k in range(4)]
    greeted += [at(c, z, xk(k), y) for k in range(1, 4)]
    greeted += [at(c, z, x, yk(k)) for k in range(1, 4)]
    greeted += [at(core, zk(way), x, y) for core in range(2) for way in (1, -1)]
    for device in greeted:
        pl.semaphore_signal(barrier, inc=1, device_id=device, device_id_type=MESH)
    pl.semaphore_wait(barrier, len(greeted))

    loads[0].wait()
    CN[z, pl.ds(0, 96)] = conn[pl.ds(0, 96)]
    CN[z, pl.ds(96, 16)] = jnp.zeros((16, 1024), BF)
    CN[z, pl.ds(96, 4)] = conn[pl.ds(96, 4)]

    def kind(item):
        return 0 if item == 0 else 2 - item % 2

    def rows_of(item, zz, start, size):
        s = (item - 1) // 2
        if item == 0:
            return CN.at[zz, pl.ds(start, size)]
        if item % 2 == 1:
            return WQ.at[s, pl.ds(pl.multiple_of(zz * 128 + start, 32), size)]
        return WO.at[s, pl.ds(start, size), pl.ds(pl.multiple_of(zz * 128, 128), 128)]

    def block(item, zz):
        return rows_of(item, zz, 0, WHOLE[kind(item)])

    def own_copy(s, n):
        ref = block(1 + 2 * s + n, z)
        return remote(ref, ref, own_s.at[n], own_r.at[n], at(1 - s, z, x, y))

    def piece_ways(item, step):
        count = len(PIECES[kind(item)])
        return [(p, w) for p in range(count) for w in range(2) if step < 4 or p // (count // 2) == w]

    def piece_copy(item, step, piece, way, arriving):
        hops = step if arriving else step - 1
        zz = zk(-hops) if way == 0 else zk(hops)
        ref = rows_of(item, zz, *PIECES[kind(item)][piece])
        target = at(1 if step < 4 else 0, zk(1) if way == 0 else zk(-1), x, y)
        arrived = z_r.at[item % 3, step - 1, way, piece] if step < 4 else f_r.at[item]
        return remote(ref, ref, z_s.at[item], arrived, target)

    def blocks(item, count):
        s = (item - 1) // 2
        if item == 0:
            return CN.at[pl.ds(0, count), pl.ds(0, 112)]
        if item % 2 == 1:
            return WQ.at[s, pl.ds(0, 128 * count)]
        return WO.at[s, :, pl.ds(0, 128 * count)]

    def waits(ref, semaphore):
        return remote(ref, ref, semaphore, semaphore, at(1 - c, z, x, y))

    def hand_over(item, index):
        step = index // 2 + 1
        zz = zk(-step) if index % 2 == 0 else zk(step)
        ref = block(item, zz)
        return remote(ref, ref, f_s.at[item], f_r.at[item], at(0, z, x, y))

    def patch_copy(k):
        return remote(PNS.at[xk(k)], PN.at[x, :, c], p_s.at[0], p_r.at[c], at(0, z, xk(k), y))

    def normed_patches():
        values = patches[...].reshape(64, 3200).astype(F32)
        centered = values - jnp.sum(values, axis=-1, keepdims=True) / 3200.0
        variance = jnp.sum(centered * centered, axis=-1, keepdims=True) / 3200.0
        normed = centered * lax.rsqrt(variance + 1e-06)
        row = lax.broadcasted_iota(jnp.int32, (64, 1), 0)
        limit = jnp.where(row < 32, tokens[0], tokens[1])
        normed = jnp.where(c * 32 + lax.rem(row, 32) < limit, normed, 0.0)
        lane = lax.broadcasted_iota(jnp.int32, (64, 128), 1)
        for j in range(32):
            zz, xx = divmod(j, NX)
            base = (100 * j) // 128 * 128
            offset = 100 * j - base
            width = 128 if offset + 100 <= 128 else 256
            window = normed[:, base : base + width]
            if offset:
                window = pltpu.roll(window, width - offset, 1)
            part = jnp.where(lane < 100, window[:, :128], 0.0)
            PNS[xx, :, :, zz * 128 : (zz + 1) * 128] = part.astype(BF).reshape(2, 32, 128)

    @pl.when(c == 1)
    def _():
        for piece, way in piece_ways(0, 1):
            piece_copy(0, 1, piece, way, False).start()
        for load in loads[1:]:
            load.wait()
        own = [own_copy(1, 0), own_copy(1, 1)]
        for copy in own:
            copy.start()
        normed_patches()
        for k in range(4):
            patch_copy(k).start()
        own_copy(0, 0).wait_recv()
        for way in range(2):
            piece_copy(1, 1, 0, way, False).start()
        for item, step in RING:
            if step == 1:
                if item == 2:
                    own_copy(0, 1).wait_recv()
                for piece, way in piece_ways(item, 1):
                    piece_copy(item, 1, piece, way, False).start()
            else:
                onward = piece_ways(item, step)
                for piece, way in piece_ways(item, step - 1):
                    piece_copy(item, step - 1, piece, way, True).wait_recv()
                    if (piece, way) in onward:
                        piece_copy(item, step, piece, way, False).start()
                if item == 0:
                    for way in range(2):
                        piece_copy(1, 1, step - 1, way, False).start()
                for index in (2 * step - 4, 2 * step - 3):
                    hand_over(item, index).start()
        for copy in own:
            copy.wait_send()
        waits(PNS, p_s.at[0]).wait_send()
        for item in range(5):
            waits(blocks(item, 7), z_s.at[item]).wait_send()
            waits(blocks(item, 6), f_s.at[item]).wait_send()

    def wait_item(item):
        waits(blocks(item, 7), f_r.at[item]).wait_recv()

    def text_copy(half, k):
        target = at(0, z, xk(k), y)
        if half == 1:
            return remote(TS.at[xk(k), :, 1], H.at[0, :, 1, y, x], t_s.at[0], t_r.at[1], target)
        return remote(TS.at[xk(k), :, 0], T0.at[:, x], t_s.at[0], t_r.at[0], target)

    def text_arrival(half):
        waits(H.at[0, :, 1, y, pl.ds(0, 3)] if half == 1 else T0.at[:, pl.ds(0, 3)], t_r.at[half]).wait_recv()

    def image_copy(b, k):
        return remote(IS.at[b, xk(k)], IR.at[b, x], i_s.at[0], i_r.at[b], at(0, z, xk(k), y))

    def image_arrival(b):
        waits(IR.at[b, pl.ds(0, 3)], i_r.at[b]).wait_recv()

    def hidden_copy(s, b, h, k):
        ref = H.at[s, b, h, y]
        return remote(ref, ref, h_s.at[0], h_r.at[b, h], at(0, z, x, yk(k)))

    def hidden_arrival(s, b, h):
        waits(H.at[s, b, h, pl.ds(0, 3)], h_r.at[b, h]).wait_recv()

    def qkv_copy(s, b, h, k, part):
        rows = pl.ds(0, 384) if part == 0 else pl.ds(384, 400)
        return remote(
            QS.at[s, b, h, xk(k), rows], QR.at[s, b, h, x, rows], q_s.at[0], q_r.at[b, h], at(0, z, xk(k), y)
        )

    def qkv_arrival(s, b, h):
        waits(QR.at[s, b, h, pl.ds(0, 3)], q_r.at[b, h]).wait_recv()

    def attended_copy(s, b, h, k):
        ref = AR.at[s, b, h, x]
        return remote(ref, ref, a_s.at[0], a_r.at[b, h], at(0, z, xk(k), y))

    def attended_arrival(s, b, h):
        waits(AR.at[s, b, h, pl.ds(0, 3)], a_r.at[b, h]).wait_recv()

    def update_copy(s, b, h, k):
        return remote(OS.at[s, b, h, yk(k)], OR.at[s, b, h, y], o_s.at[0], o_r.at[b, h], at(0, z, x, yk(k)))

    def update_arrival(s, b, h):
        waits(OR.at[s, b, h, pl.ds(0, 3)], o_r.at[b, h]).wait_recv()

    def final_copy(b, h, k):
        return remote(FS.at[b, h, xk(k)], FR.at[x, b], e_s.at[h], e_r.at[b], at(h, z, xk(k), y))

    def send_text():
        position = lax.broadcasted_iota(jnp.int32, (128, 1), 0)
        for b in range(2):
            masked = jnp.where(position < tokens[b], jnp.zeros_like(text[b]), text[b])
            for xx in range(NX):
                for zz in range(2):
                    lanes = zz * 512 + xx * 128
                    TS[xx, b, :, :, zz * 128 : (zz + 1) * 128] = masked[:, lanes : lanes + 128].reshape(2, 64, 128)
        for b in range(2):
            H[0, b, 1, y, x] = TS[x, b, 1]
            T0[b, x] = TS[x, b, 0]
        for half in (1, 0):
            for k in range(1, 4):
                text_copy(half, k).start()

    def image_part():
        waits(PN.at[pl.ds(0, 3), :, 0], p_r.at[0]).wait_recv()
        waits(PN.at[:, :, 1], p_r.at[1]).wait_recv()
        wait_item(0)
        for b in range(2):
            rows = PN[:, b].reshape(256, 1024)
            for zz in range(2):
                for pair in range(2):
                    lanes = zz * 512 + pair * 256
                    product = jnp.dot(
                        rows, CN[:, :, lanes : lanes + 256].reshape(1024, 256), preferred_element_type=F32
                    ).astype(BF)
                    for n in range(2):
                        part = product[:, n * 128 : (n + 1) * 128]
                        IS[b, 2 * pair + n, :, :, zz * 128 : (zz + 1) * 128] = part.reshape(4, 64, 128)
            for k in range(1, 4):
                image_copy(b, k).start()
        text_arrival(0)
        for b in range(2):
            image_arrival(b)
            total = IS[b, x].astype(F32)
            for k in range(1, 4):
                total = total + IR[b, xk(k)].astype(F32)
            H[0, b, 0, y] = (total.astype(BF).astype(F32) + T0[b].astype(F32)).astype(BF)
            for k in range(1, 4):
                hidden_copy(0, b, 0, k).start()

    def project(s, b, h):
        squares = jnp.zeros((256, 256), F32)
        for q in range(4):
            values = H[s, b, h, q].reshape(256, 256).astype(F32)
            squares = squares + values * values
        squares = jnp.sum(squares, axis=-1, keepdims=True)
        high = squares.astype(BF).astype(F32)
        row = lax.rem(lax.broadcasted_iota(jnp.int32, (256, 128), 0), 64)
        lane = lax.broadcasted_iota(jnp.int32, (256, 128), 1)
        spread = jnp.where(lane == row, high, jnp.where(lane == row + 64, squares - high, 0.0))
        spread = jnp.sum(spread.reshape(4, 64, 128), axis=1, keepdims=True)
        QS[s, b, h, :, 768:784, :] = jnp.broadcast_to(spread, (4, 16, 128)).astype(BF)

        def tile(n, _):
            lanes = pl.ds(pl.multiple_of(n * 256, 256), 256)
            total = jnp.zeros((256, 256), F32)
            for q in range(4):
                total = total + jnp.dot(
                    H[s, b, h, q].reshape(256, 256),
                    WQ[s, pl.ds(q * 256, 256), lanes],
                    preferred_element_type=F32,
                )
            for i in range(2):
                rows = pl.ds(pl.multiple_of((2 * n + i) * 64, 64), 64)
                QS[s, b, h, :, rows, :] = total[:, i * 128 : (i + 1) * 128].astype(BF).reshape(4, 64, 128)

            @pl.when(n == 2)
            def _():
                for k in range(1, 4):
                    qkv_copy(s, b, h, k, 0).start()

            return 0

        lax.fori_loop(0, 6, tile, 0)
        for k in range(1, 4):
            qkv_copy(s, b, h, k, 1).start()

    def attend(s, b, h):
        qkv_arrival(s, b, h)

        def summed(start, size=64):
            rows = slice(start, start + size)
            total = QS[s, b, h, x, rows].astype(F32)
            for k in range(1, 4):
                total = total + QR[s, b, h, xk(k), rows].astype(F32)
            return total

        row = lax.broadcasted_iota(jnp.int32, (64, 128), 0)
        lane = lax.broadcasted_iota(jnp.int32, (64, 128), 1)
        spread = jnp.where(lax.rem(lane, 64) == row, summed(768, 16)[0:1], 0.0)
        squares = jnp.sum(spread, axis=-1, keepdims=True)
        scale = lax.rsqrt(squares / 4096.0 + 1e-05)
        half = pl.ds(pl.multiple_of(h * 64, 64), 64)
        cos_rows = cosine[half]
        sin_rows = sine[half]

        def rotated(start):
            rows = summed(start) * scale
            return (rows * cos_rows + pltpu.roll(rows, 64, 1) * sin_rows).astype(BF)

        row = lax.rem(lax.broadcasted_iota(jnp.int32, (256, 128), 0), 64) + h * 64
        column = lax.broadcasted_iota(jnp.int32, (256, 128), 1)
        for g in range(2):
            KS[b, g, half] = rotated((8 + g) * 64)
            VS[b, g, half] = (summed((10 + g) * 64) * scale).astype(BF)
            stacked = jnp.concatenate([rotated((4 * g + j) * 64) for j in range(4)], axis=0)
            scores = lax.dot_general(
                stacked, KS[b, g], (((1,), (1,)), ((), ())), preferred_element_type=F32
            )
            scores = jnp.where(row >= column, scores * SCALE, -1e30)
            weights = jnp.exp(scores - jnp.max(scores, axis=-1, keepdims=True))
            norm = jnp.sum(weights, axis=-1, keepdims=True)
            mixed = jnp.dot(weights.astype(BF), VS[b, g], preferred_element_type=F32) / norm
            for j in range(4):
                lanes = (4 * g + j) * 128
                AR[s, b, h, x, :, lanes : lanes + 128] = mixed[j * 64 : (j + 1) * 64].astype(BF)
        for k in range(1, 4):
            attended_copy(s, b, h, k).start()

    def update(s, b, h):
        attended_arrival(s, b, h)

        def tile(n, _):
            yd = yk(n + 1)
            lanes = pl.ds(pl.multiple_of(yd * 256, 256), 256)
            product = jnp.dot(AR[s, b, h].reshape(256, 1024), WO[s, :, lanes], preferred_element_type=F32)
            OS[s, b, h, yd] = product.astype(BF).reshape(4, 64, 256)

            @pl.when(n < 3)
            def _():
                update_copy(s, b, h, n + 1).start()

            return 0

        lax.fori_loop(0, 4, tile, 0)

    def renew(s, b, h):
        update_arrival(s, b, h)
        total = OS[s, b, h, y].astype(F32)
        for k in range(1, 4):
            total = total + OR[s, b, h, yk(k)].astype(F32)
        fresh = (H[s, b, h, y].astype(F32) + total).astype(BF)

        @pl.when(s == 0)
        def _():
            H[1, b, h, y] = fresh
            for k in range(1, 4):
                hidden_copy(1, b, h, k).start()

        @pl.when(s == 1)
        def _():
            FS[b, h] = fresh
            for k in range(1, 4):
                final_copy(b, h, k).start()

            @pl.when(h == 0)
            def _():
                FR[x, b] = FS[b, 0, x]

            @pl.when(h == 1)
            def _():
                final_copy(b, h, 0).start()

    @pl.when(c == 0)
    def _():
        for load in loads[1:4]:
            load.wait()
        own_copy(0, 0).start()
        for load in loads[4:]:
            load.wait()
        own_copy(0, 1).start()
        send_text()
        for zz in range(NZ):
            CN[zz, pl.ds(112, 16)] = jnp.zeros((16, 1024), BF)
        KS[...] = jnp.zeros_like(KS)
        VS[...] = jnp.zeros_like(VS)
        normed_patches()
        PN[x, :, 0] = PNS[x]
        for k in range(1, 4):
            patch_copy(k).start()
        text_arrival(1)
        for b in range(2):
            for k in range(1, 4):
                hidden_copy(0, b, 1, k).start()
        image_part()

        def stage(n, word):
            fresh = jnp.int32(WORDS[7])
            for m in range(7):
                fresh = jnp.where(lax.div(n, 4) == m, jnp.int32(WORDS[m]), fresh)
            word = jnp.where(lax.rem(n, 4) == 0, fresh, word)
            code = lax.rem(word, 32)
            what = lax.div(code, 8)
            s = lax.rem(lax.div(code, 4), 2)
            b = lax.rem(lax.div(code, 2), 2)
            h = lax.rem(code, 2)

            for item in range(1, 5):

                @pl.when(n == FIRST[item])
                def _():
                    if item > 2:
                        own_copy(1, item - 3).wait_recv()
                    wait_item(item)

            @pl.when(what == PROJECT)
            def _():
                hidden_arrival(s, b, h)
                project(s, b, h)

            @pl.when(what == ATTEND)
            def _():
                attend(s, b, h)

            @pl.when(what == UPDATE)
            def _():
                update(s, b, h)

            @pl.when(what == RENEW)
            def _():
                renew(s, b, h)

            return lax.div(word, 32)

        lax.fori_loop(0, 32, stage, jnp.int32(0))

    for b in range(2):

        @pl.when(c == 0)
        def _():
            waits(FR.at[pl.ds(0, 3), b], e_r.at[b]).wait_recv()

        @pl.when(c == 1)
        def _():
            waits(FR.at[:, b], e_r.at[b]).wait_recv()

    for b in range(2):
        for xx in range(NX):
            for zz in range(2):
                lanes = zz * 512 + xx * 128
                out[b, :, lanes : lanes + 128] = FR[xx, b, :, zz * 128 : (zz + 1) * 128]

    @pl.when(c == 0)
    def _():
        own_copy(0, 0).wait_send()
        own_copy(0, 1).wait_send()
        waits(PNS.at[pl.ds(0, 3)], p_s.at[0]).wait_send()
        waits(TS.at[pl.ds(0, 3)], t_s.at[0]).wait_send()
        waits(IS.at[:, pl.ds(0, 3)], i_s.at[0]).wait_send()
        for sent, semaphore in ((H, h_s), (QS, q_s), (AR, a_s), (OS, o_s)):
            waits(sent.at[:, :, :, pl.ds(0, 3)], semaphore.at[0]).wait_send()
        waits(FS.at[:, 0, pl.ds(0, 3)], e_s.at[0]).wait_send()
        waits(FS.at[:, 1], e_s.at[1]).wait_send()


def rotation_tables():
    frequencies = 500000.0 ** (-(np.arange(64, dtype=np.float32) * np.float32(2.0) / np.float32(128)))
    angles = np.arange(128, dtype=np.float32)[:, None] * frequencies.astype(np.float32)[None, :]
    cosine, sine = np.cos(angles), np.sin(angles)
    return (
        np.concatenate([cosine, cosine], axis=1).astype(np.float32),
        np.concatenate([-sine, sine], axis=1).astype(np.float32),
    )


def shards(text_embeds, patches, image_tokens, connector, w_query, w_keyval, w_out):
    cosine, sine = rotation_tables()
    vmem = pl.BlockSpec(memory_space=pltpu.VMEM)
    dma = pltpu.SemaphoreType.DMA
    return pl.pallas_call(
        kernel,
        out_shape=jax.ShapeDtypeStruct((2, 64, 1024), BF),
        in_specs=[pl.BlockSpec(memory_space=pl.ANY)] * 9,
        out_specs=vmem,
        scratch_shapes=[
            pltpu.VMEM((2, 128, 1024), BF),
            pltpu.VMEM((2, 32, 3200), BF),
            pltpu.SMEM((2,), jnp.int32),
            pltpu.VMEM((100, 1024), BF),
            pltpu.VMEM((128, 128), F32),
            pltpu.VMEM((128, 128), F32),
            pltpu.VMEM((8, 128, 1024), BF),
            pltpu.VMEM((2, 1024, 1536), BF),
            pltpu.VMEM((2, 1024, 1024), BF),
            pltpu.VMEM((4, 2, 32, 1024), BF),
            pltpu.VMEM((4, 2, 2, 32, 1024), BF),
            pltpu.VMEM((4, 2, 2, 64, 256), BF),
            pltpu.VMEM((2, 4, 64, 256), BF),
            pltpu.VMEM((2, 4, 4, 64, 256), BF),
            pltpu.VMEM((2, 4, 4, 64, 256), BF),
            pltpu.VMEM((2, 2, 2, 4, 4, 64, 256), BF),
            pltpu.VMEM((2, 2, 2, 4, 784, 128), BF),
            pltpu.VMEM((2, 2, 2, 4, 784, 128), BF),
            pltpu.VMEM((2, 2, 128, 128), BF),
            pltpu.VMEM((2, 2, 128, 128), BF),
            pltpu.VMEM((2, 2, 2, 4, 64, 1024), BF),
            pltpu.VMEM((2, 2, 2, 4, 4, 64, 256), BF),
            pltpu.VMEM((2, 2, 2, 4, 4, 64, 256), BF),
            pltpu.VMEM((2, 2, 4, 64, 256), BF),
            pltpu.VMEM((4, 2, 64, 256), BF),
            dma((10,)),
            dma((2,)), dma((2,)),
            dma((5,)), dma((3, 3, 2, 4)),
            dma((5,)), dma((5,)),
            dma((1,)), dma((2,)),
            dma((1,)), dma((2,)),
            dma((1,)), dma((2,)),
            dma((1,)), dma((2, 2)),
            dma((1,)), dma((2, 2)),
            dma((1,)), dma((2, 2)),
            dma((1,)), dma((2, 2)),
            dma((2,)), dma((2,)),
        ],
        compiler_params=pltpu.CompilerParams(
            collective_id=0, has_side_effects=True, vmem_limit_bytes=62 * 2**20
        ),
        cost_estimate=pl.CostEstimate(flops=11 * 10**9, bytes_accessed=20 * 10**6, transcendentals=10**6),
        name="decoder",
    )(text_embeds, patches, image_tokens, connector, w_query, w_keyval, w_out, cosine, sine)


def solution(mesh):
    placed = (
        P("dp", None, "tensor"),
        P("dp", "pipe", None),
        P("dp"),
        P("dp", "tensor"),
        P("pipe", "dp", "tensor"),
        P("pipe", None, "dp", "tensor"),
        P("pipe", "tensor", "dp"),
    )
    return jax.shard_map(
        shards, mesh=mesh, in_specs=placed, out_specs=P("dp", "pipe", "tensor"), check_vma=False
    )
```

```python
import math

import jax
import jax.numpy as jnp
import numpy as np
from jax import lax
from jax.experimental import pallas as pl
from jax.experimental.pallas import tpu as pltpu
from jax.sharding import PartitionSpec as P

MESH = pl.DeviceIdType.MESH
BF = jnp.bfloat16
F32 = jnp.float32
NX, NY, NZ = 4, 4, 8
SCALE = 1.0 / math.sqrt(128)
FAR_FIRST = (2, 1, 3)

RING = [
    (0, 2), (0, 3), (0, 4), (1, 2), (1, 3), (1, 4), (2, 1), (2, 2), (2, 3), (3, 1), (2, 4),
    (3, 2), (3, 3), (4, 1), (3, 4), (4, 2), (4, 3), (4, 4),
]
PIECES = (((0, 32), (32, 32), (64, 32), (96, 16)), ((0, 32), (32, 32), (64, 32), (96, 32)), ((0, 512), (512, 512)))
WHOLE = (112, 128, 1024)

PROJECT, ATTEND, UPDATE, RENEW = range(4)
CODES = (
    1, 0, 2, 8, 9, 3, 16, 10, 17, 24, 11, 25, 18, 4, 19, 5, 26, 27, 12, 6, 13, 20, 7, 21, 14, 15, 22, 23, 28, 29, 30, 31,
)
AWAITED = {8 * PROJECT: 1, 8 * PROJECT + 4: 3, 8 * UPDATE: 2, 8 * UPDATE + 4: 4}
FIRST = {item: min(n for n, code in enumerate(CODES) if code // 4 == at // 4) for at, item in AWAITED.items()}
WORDS = [sum(code << (5 * n) for n, code in enumerate(CODES[i : i + 4])) for i in range(0, 32, 4)]


def remote(src, dst, send_sem, recv_sem, device):
    return pltpu.make_async_remote_copy(
        src_ref=src,
        dst_ref=dst,
        send_sem=send_sem,
        recv_sem=recv_sem,
        device_id=device,
        device_id_type=MESH,
    )


def kernel(
    text_in, patches_in, tokens_in, conn_in, wq, wkv, wo, cosine_in, sine_in, out,
    text, patches, tokens, conn, cosine, sine,
    CN, WQ, WO, PNS, PN, TS, T0, IS, IR, H, QS, QR, KS, VS, AR, OS, OR, FS, FR,
    l_s, own_s, own_r, z_s, z_r, f_s, f_r, p_s, p_r, t_s, t_r, i_s, i_r,
    h_s, h_r, q_s, q_r, a_s, a_r, o_s, o_r, e_s, e_r,
):
    c = lax.axis_index("pipe")
    d = lax.axis_index("dp")
    y = lax.axis_index("tensor")
    z = lax.div(d, NX)
    x = lax.rem(d, NX)

    def at(core, zz, xx, yy):
        return (core, zz * NX + xx, yy)

    def xk(k):
        return lax.rem(x + k, NX)

    def yk(k):
        return lax.rem(y + k, NY)

    def zk(k):
        return lax.rem(z + k + NZ, NZ)

    zrow = pl.multiple_of(z * 128, 128)
    local = [
        (conn_in, conn),
        (wq.at[0], WQ.at[c, pl.ds(zrow, 128), pl.ds(0, 1024)]),
        (wkv.at[0, 0], WQ.at[c, pl.ds(zrow, 128), pl.ds(1024, 256)]),
        (wkv.at[0, 1], WQ.at[c, pl.ds(zrow, 128), pl.ds(1280, 256)]),
        (patches_in, patches),
        (tokens_in, tokens),
        (text_in, text),
        (wo.at[0], WO.at[c, :, pl.ds(zrow, 128)]),
        (cosine_in, cosine),
        (sine_in, sine),
    ]
    loads = [pltpu.make_async_copy(a, b, l_s.at[n]) for n, (a, b) in enumerate(local)]
    for load in loads:
        load.start()

    barrier = pltpu.get_barrier_semaphore()
    both = [at(1 - c, z, xk(k), y) for k in range(4)] + [at(1 - c, zk(way), x, y) for way in (1, -1)]
    plane = [at(0, z, xk(k), y) for k in range(1, 4)] + [at(0, z, x, yk(k)) for k in range(1, 4)]
    line = [at(1, zk(way), x, y) for way in (1, -1)]

    def greet(devices):
        for device in devices:
            pl.semaphore_signal(barrier, inc=1, device_id=device, device_id_type=MESH)

    greet(both)

    @pl.when(c == 0)
    def _():
        greet(plane)
        pl.semaphore_wait(barrier, len(both) + len(plane))

    @pl.when(c == 1)
    def _():
        greet(line)
        pl.semaphore_wait(barrier, len(both) + len(line))

    loads[0].wait()
    CN[z, pl.ds(0, 96)] = conn[pl.ds(0, 96)]
    CN[z, pl.ds(96, 16)] = jnp.zeros((16, 1024), BF)
    CN[z, pl.ds(96, 4)] = conn[pl.ds(96, 4)]

    def kind(item):
        return 0 if item == 0 else 2 - item % 2

    def rows_of(item, zz, start, size):
        s = (item - 1) // 2
        if item == 0:
            return CN.at[zz, pl.ds(start, size)]
        if item % 2 == 1:
            return WQ.at[s, pl.ds(pl.multiple_of(zz * 128 + start, 32), size)]
        return WO.at[s, pl.ds(start, size), pl.ds(pl.multiple_of(zz * 128, 128), 128)]

    def block(item, zz):
        return rows_of(item, zz, 0, WHOLE[kind(item)])

    def own_copy(s, n):
        ref = block(1 + 2 * s + n, z)
        return remote(ref, ref, own_s.at[n], own_r.at[n], at(1 - s, z, x, y))

    def piece_ways(item, step):
        count = len(PIECES[kind(item)])
        return [(p, w) for p in range(count) for w in range(2) if step < 4 or p // (count // 2) == w]

    def piece_copy(item, step, piece, way, arriving):
        hops = step if arriving else step - 1
        zz = zk(-hops) if way == 0 else zk(hops)
        ref = rows_of(item, zz, *PIECES[kind(item)][piece])
        target = at(1 if step < 4 else 0, zk(1) if way == 0 else zk(-1), x, y)
        arrived = z_r.at[item % 3, step - 1, way, piece] if step < 4 else f_r.at[item]
        return remote(ref, ref, z_s.at[item], arrived, target)

    def blocks(item, count):
        s = (item - 1) // 2
        if item == 0:
            return CN.at[pl.ds(0, count), pl.ds(0, 112)]
        if item % 2 == 1:
            return WQ.at[s, pl.ds(0, 128 * count)]
        return WO.at[s, :, pl.ds(0, 128 * count)]

    def waits(ref, semaphore):
        return remote(ref, ref, semaphore, semaphore, at(1 - c, z, x, y))

    def hand_over(item, index):
        step = index // 2 + 1
        zz = zk(-step) if index % 2 == 0 else zk(step)
        ref = block(item, zz)
        return remote(ref, ref, f_s.at[item], f_r.at[item], at(0, z, x, y))

    def patch_copy(k):
        return remote(PNS.at[xk(k)], PN.at[x, :, c], p_s.at[0], p_r.at[c], at(0, z, xk(k), y))

    def normed_patches():
        values = patches[...].reshape(64, 3200).astype(F32)
        centered = values - jnp.sum(values, axis=-1, keepdims=True) / 3200.0
        variance = jnp.sum(centered * centered, axis=-1, keepdims=True) / 3200.0
        normed = centered * lax.rsqrt(variance + 1e-06)
        row = lax.broadcasted_iota(jnp.int32, (64, 1), 0)
        limit = jnp.where(row < 32, tokens[0], tokens[1])
        normed = jnp.where(c * 32 + lax.rem(row, 32) < limit, normed, 0.0)
        lane = lax.broadcasted_iota(jnp.int32, (64, 128), 1)
        for j in range(32):
            zz, xx = divmod(j, NX)
            base = (100 * j) // 128 * 128
            offset = 100 * j - base
            width = 128 if offset + 100 <= 128 else 256
            window = normed[:, base : base + width]
            if offset:
                window = pltpu.roll(window, width - offset, 1)
            part = jnp.where(lane < 100, window[:, :128], 0.0)
            PNS[xx, :, :, zz * 128 : (zz + 1) * 128] = part.astype(BF).reshape(2, 32, 128)

    @pl.when(c == 1)
    def _():
        for piece, way in piece_ways(0, 1):
            piece_copy(0, 1, piece, way, False).start()
        for load in loads[1:]:
            load.wait()
        own = [own_copy(1, 0), own_copy(1, 1)]
        for copy in own:
            copy.start()
        normed_patches()
        for k in range(4):
            patch_copy(k).start()
        own_copy(0, 0).wait_recv()
        for way in range(2):
            piece_copy(1, 1, 0, way, False).start()
        for item, step in RING:
            if step == 1:
                if item == 2:
                    own_copy(0, 1).wait_recv()
                for piece, way in piece_ways(item, 1):
                    piece_copy(item, 1, piece, way, False).start()
            else:
                onward = piece_ways(item, step)
                for piece, way in piece_ways(item, step - 1):
                    piece_copy(item, step - 1, piece, way, True).wait_recv()
                    if (piece, way) in onward:
                        piece_copy(item, step, piece, way, False).start()
                if item == 0:
                    for way in range(2):
                        piece_copy(1, 1, step - 1, way, False).start()
                for index in (2 * step - 4, 2 * step - 3):
                    hand_over(item, index).start()
        for copy in own:
            copy.wait_send()
        waits(PNS, p_s.at[0]).wait_send()
        for item in range(5):
            waits(blocks(item, 7), z_s.at[item]).wait_send()
            waits(blocks(item, 6), f_s.at[item]).wait_send()

    def wait_item(item):
        waits(blocks(item, 7), f_r.at[item]).wait_recv()

    def text_copy(half, k):
        target = at(0, z, xk(k), y)
        if half == 1:
            return remote(TS.at[xk(k), :, 1], H.at[0, :, 1, y, x], t_s.at[0], t_r.at[1], target)
        return remote(TS.at[xk(k), :, 0], T0.at[:, x], t_s.at[0], t_r.at[0], target)

    def text_arrival(half):
        waits(H.at[0, :, 1, y, pl.ds(0, 3)] if half == 1 else T0.at[:, pl.ds(0, 3)], t_r.at[half]).wait_recv()

    def image_copy(b, k):
        return remote(IS.at[b, xk(k)], IR.at[b, x], i_s.at[0], i_r.at[b], at(0, z, xk(k), y))

    def image_arrival(b):
        waits(IR.at[b, pl.ds(0, 3)], i_r.at[b]).wait_recv()

    def hidden_copy(s, b, h, k):
        ref = H.at[s, b, h, y]
        return remote(ref, ref, h_s.at[0], h_r.at[b, h], at(0, z, x, yk(k)))

    def hidden_arrival(s, b, h):
        waits(H.at[s, b, h, pl.ds(0, 3)], h_r.at[b, h]).wait_recv()

    def qkv_copy(s, b, h, k, part):
        rows = pl.ds(0, 384) if part == 0 else pl.ds(384, 400)
        return remote(
            QS.at[s, b, h, xk(k), rows], QR.at[s, b, h, x, rows], q_s.at[0], q_r.at[b, h], at(0, z, xk(k), y)
        )

    def qkv_arrival(s, b, h):
        waits(QR.at[s, b, h, pl.ds(0, 3)], q_r.at[b, h]).wait_recv()

    def attended_copy(s, b, h, k, g):
        ref = AR.at[s, b, h, x, :, pl.ds(g * 512, 512)]
        return remote(ref, ref, a_s.at[0], a_r.at[b, h], at(0, z, xk(k), y))

    def attended_arrival(s, b, h):
        waits(AR.at[s, b, h, pl.ds(0, 3)], a_r.at[b, h]).wait_recv()

    def update_copy(s, b, h, k):
        return remote(OS.at[s, b, h, yk(k)], OR.at[s, b, h, y], o_s.at[0], o_r.at[b, h], at(0, z, x, yk(k)))

    def update_arrival(s, b, h):
        waits(OR.at[s, b, h, pl.ds(0, 3)], o_r.at[b, h]).wait_recv()

    def final_copy(b, h, k):
        return remote(FS.at[b, h, xk(k)], FR.at[x, b], e_s.at[h], e_r.at[b], at(h, z, xk(k), y))

    def send_text():
        position = lax.broadcasted_iota(jnp.int32, (128, 1), 0)
        for b in range(2):
            masked = jnp.where(position < tokens[b], jnp.zeros_like(text[b]), text[b])
            for xx in range(NX):
                for zz in range(2):
                    lanes = zz * 512 + xx * 128
                    TS[xx, b, :, :, zz * 128 : (zz + 1) * 128] = masked[:, lanes : lanes + 128].reshape(2, 64, 128)
        for b in range(2):
            H[0, b, 1, y, x] = TS[x, b, 1]
            T0[b, x] = TS[x, b, 0]
        for half in (1, 0):
            for k in FAR_FIRST:
                text_copy(half, k).start()

    def image_part():
        waits(PN.at[pl.ds(0, 3), :, 0], p_r.at[0]).wait_recv()
        waits(PN.at[:, :, 1], p_r.at[1]).wait_recv()
        wait_item(0)
        for b in range(2):
            rows = PN[:, b].reshape(256, 1024)
            for zz in range(2):
                for pair in range(2):
                    lanes = zz * 512 + pair * 256
                    product = jnp.dot(
                        rows, CN[:, :, lanes : lanes + 256].reshape(1024, 256), preferred_element_type=F32
                    ).astype(BF)
                    for n in range(2):
                        part = product[:, n * 128 : (n + 1) * 128]
                        IS[b, 2 * pair + n, :, :, zz * 128 : (zz + 1) * 128] = part.reshape(4, 64, 128)
            for k in FAR_FIRST:
                image_copy(b, k).start()
        text_arrival(0)
        for b in range(2):
            image_arrival(b)
            total = IS[b, x].astype(F32)
            for k in FAR_FIRST:
                total = total + IR[b, xk(k)].astype(F32)
            H[0, b, 0, y] = (total.astype(BF).astype(F32) + T0[b].astype(F32)).astype(BF)
            for k in FAR_FIRST:
                hidden_copy(0, b, 0, k).start()

    def project(s, b, h):
        squares = jnp.zeros((256, 256), F32)
        for q in range(4):
            values = H[s, b, h, q].reshape(256, 256).astype(F32)
            squares = squares + values * values
        squares = jnp.sum(squares, axis=-1, keepdims=True)
        high = squares.astype(BF).astype(F32)
        row = lax.rem(lax.broadcasted_iota(jnp.int32, (256, 128), 0), 64)
        lane = lax.broadcasted_iota(jnp.int32, (256, 128), 1)
        spread = jnp.where(lane == row, high, jnp.where(lane == row + 64, squares - high, 0.0))
        spread = jnp.sum(spread.reshape(4, 64, 128), axis=1, keepdims=True)
        QS[s, b, h, :, 768:784, :] = jnp.broadcast_to(spread, (4, 16, 128)).astype(BF)

        def tile(n, _):
            lanes = pl.ds(pl.multiple_of(n * 256, 256), 256)
            total = jnp.zeros((256, 256), F32)
            for q in range(4):
                total = total + jnp.dot(
                    H[s, b, h, q].reshape(256, 256),
                    WQ[s, pl.ds(q * 256, 256), lanes],
                    preferred_element_type=F32,
                )
            for i in range(2):
                rows = pl.ds(pl.multiple_of((2 * n + i) * 64, 64), 64)
                QS[s, b, h, :, rows, :] = total[:, i * 128 : (i + 1) * 128].astype(BF).reshape(4, 64, 128)

            @pl.when(n == 2)
            def _():
                for k in FAR_FIRST:
                    qkv_copy(s, b, h, k, 0).start()

            return 0

        lax.fori_loop(0, 6, tile, 0)
        for k in FAR_FIRST:
            qkv_copy(s, b, h, k, 1).start()

    def attend(s, b, h):
        qkv_arrival(s, b, h)

        def summed(start, size=64):
            rows = slice(start, start + size)
            total = QS[s, b, h, x, rows].astype(F32)
            for k in FAR_FIRST:
                total = total + QR[s, b, h, xk(k), rows].astype(F32)
            return total

        row = lax.broadcasted_iota(jnp.int32, (64, 128), 0)
        lane = lax.broadcasted_iota(jnp.int32, (64, 128), 1)
        spread = jnp.where(lax.rem(lane, 64) == row, summed(768, 16)[0:1], 0.0)
        squares = jnp.sum(spread, axis=-1, keepdims=True)
        scale = lax.rsqrt(squares / 4096.0 + 1e-05)
        half = pl.ds(pl.multiple_of(h * 64, 64), 64)
        cos_rows = cosine[half]
        sin_rows = sine[half]

        def rotated(start):
            rows = summed(start) * scale
            return (rows * cos_rows + pltpu.roll(rows, 64, 1) * sin_rows).astype(BF)

        row = lax.rem(lax.broadcasted_iota(jnp.int32, (256, 128), 0), 64) + h * 64
        column = lax.broadcasted_iota(jnp.int32, (256, 128), 1)
        for g in range(2):
            KS[b, g, half] = rotated((8 + g) * 64)
            VS[b, g, half] = (summed((10 + g) * 64) * scale).astype(BF)
            stacked = jnp.concatenate([rotated((4 * g + j) * 64) for j in range(4)], axis=0)
            scores = lax.dot_general(
                stacked, KS[b, g], (((1,), (1,)), ((), ())), preferred_element_type=F32
            )
            scores = jnp.where(row >= column, scores * SCALE, -1e30)
            weights = jnp.exp(scores - jnp.max(scores, axis=-1, keepdims=True))
            norm = jnp.sum(weights, axis=-1, keepdims=True)
            mixed = jnp.dot(weights.astype(BF), VS[b, g], preferred_element_type=F32) / norm
            for j in range(4):
                lanes = (4 * g + j) * 128
                AR[s, b, h, x, :, lanes : lanes + 128] = mixed[j * 64 : (j + 1) * 64].astype(BF)
            for k in FAR_FIRST:
                attended_copy(s, b, h, k, g).start()

    def update(s, b, h):
        attended_arrival(s, b, h)

        def tile(n, _):
            k = jnp.where(n == 0, 2, jnp.where(n == 1, 1, jnp.where(n == 2, 3, 0)))
            yd = yk(k)
            lanes = pl.ds(pl.multiple_of(yd * 256, 256), 256)
            product = jnp.dot(AR[s, b, h].reshape(256, 1024), WO[s, :, lanes], preferred_element_type=F32)
            OS[s, b, h, yd] = product.astype(BF).reshape(4, 64, 256)

            @pl.when(n < 3)
            def _():
                update_copy(s, b, h, k).start()

            return 0

        lax.fori_loop(0, 4, tile, 0)

    def renew(s, b, h):
        update_arrival(s, b, h)
        total = OS[s, b, h, y].astype(F32)
        for k in FAR_FIRST:
            total = total + OR[s, b, h, yk(k)].astype(F32)
        fresh = (H[s, b, h, y].astype(F32) + total).astype(BF)

        @pl.when(s == 0)
        def _():
            H[1, b, h, y] = fresh
            for k in FAR_FIRST:
                hidden_copy(1, b, h, k).start()

        @pl.when(s == 1)
        def _():
            FS[b, h] = fresh
            for k in FAR_FIRST:
                final_copy(b, h, k).start()

            @pl.when(h == 0)
            def _():
                FR[x, b] = FS[b, 0, x]

            @pl.when(h == 1)
            def _():
                final_copy(b, h, 0).start()

    @pl.when(c == 0)
    def _():
        for load in loads[1:4]:
            load.wait()
        own_copy(0, 0).start()
        for load in loads[4:]:
            load.wait()
        own_copy(0, 1).start()
        send_text()
        for zz in range(NZ):
            CN[zz, pl.ds(112, 16)] = jnp.zeros((16, 1024), BF)
        KS[...] = jnp.zeros_like(KS)
        VS[...] = jnp.zeros_like(VS)
        normed_patches()
        PN[x, :, 0] = PNS[x]
        for k in FAR_FIRST:
            patch_copy(k).start()
        text_arrival(1)
        for b in range(2):
            for k in FAR_FIRST:
                hidden_copy(0, b, 1, k).start()
        image_part()

        def stage(n, word):
            fresh = jnp.int32(WORDS[7])
            for m in range(7):
                fresh = jnp.where(lax.div(n, 4) == m, jnp.int32(WORDS[m]), fresh)
            word = jnp.where(lax.rem(n, 4) == 0, fresh, word)
            code = lax.rem(word, 32)
            what = lax.div(code, 8)
            s = lax.rem(lax.div(code, 4), 2)
            b = lax.rem(lax.div(code, 2), 2)
            h = lax.rem(code, 2)

            for item in range(1, 5):

                @pl.when(n == FIRST[item])
                def _():
                    if item > 2:
                        own_copy(1, item - 3).wait_recv()
                    wait_item(item)

            @pl.when(what == PROJECT)
            def _():
                hidden_arrival(s, b, h)
                project(s, b, h)

            @pl.when(what == ATTEND)
            def _():
                attend(s, b, h)

            @pl.when(what == UPDATE)
            def _():
                update(s, b, h)

            @pl.when(what == RENEW)
            def _():
                renew(s, b, h)

            return lax.div(word, 32)

        lax.fori_loop(0, 32, stage, jnp.int32(0))

    for b in range(2):

        @pl.when(c == 0)
        def _():
            waits(FR.at[pl.ds(0, 3), b], e_r.at[b]).wait_recv()

        @pl.when(c == 1)
        def _():
            waits(FR.at[:, b], e_r.at[b]).wait_recv()

    for b in range(2):
        for xx in range(NX):
            for zz in range(2):
                lanes = zz * 512 + xx * 128
                out[b, :, lanes : lanes + 128] = FR[xx, b, :, zz * 128 : (zz + 1) * 128]

    @pl.when(c == 0)
    def _():
        own_copy(0, 0).wait_send()
        own_copy(0, 1).wait_send()
        waits(PNS.at[pl.ds(0, 3)], p_s.at[0]).wait_send()
        waits(TS.at[pl.ds(0, 3)], t_s.at[0]).wait_send()
        waits(IS.at[:, pl.ds(0, 3)], i_s.at[0]).wait_send()
        for sent, semaphore in ((H, h_s), (QS, q_s), (AR, a_s), (OS, o_s)):
            waits(sent.at[:, :, :, pl.ds(0, 3)], semaphore.at[0]).wait_send()
        waits(FS.at[:, 0, pl.ds(0, 3)], e_s.at[0]).wait_send()
        waits(FS.at[:, 1], e_s.at[1]).wait_send()


def rotation_tables():
    frequencies = 500000.0 ** (-(np.arange(64, dtype=np.float32) * np.float32(2.0) / np.float32(128)))
    angles = np.arange(128, dtype=np.float32)[:, None] * frequencies.astype(np.float32)[None, :]
    cosine, sine = np.cos(angles), np.sin(angles)
    return (
        np.concatenate([cosine, cosine], axis=1).astype(np.float32),
        np.concatenate([-sine, sine], axis=1).astype(np.float32),
    )


def shards(text_embeds, patches, image_tokens, connector, w_query, w_keyval, w_out):
    cosine, sine = rotation_tables()
    vmem = pl.BlockSpec(memory_space=pltpu.VMEM)
    dma = pltpu.SemaphoreType.DMA
    return pl.pallas_call(
        kernel,
        out_shape=jax.ShapeDtypeStruct((2, 64, 1024), BF),
        in_specs=[pl.BlockSpec(memory_space=pl.ANY)] * 9,
        out_specs=vmem,
        scratch_shapes=[
            pltpu.VMEM((2, 128, 1024), BF),
            pltpu.VMEM((2, 32, 3200), BF),
            pltpu.SMEM((2,), jnp.int32),
            pltpu.VMEM((100, 1024), BF),
            pltpu.VMEM((128, 128), F32),
            pltpu.VMEM((128, 128), F32),
            pltpu.VMEM((8, 128, 1024), BF),
            pltpu.VMEM((2, 1024, 1536), BF),
            pltpu.VMEM((2, 1024, 1024), BF),
            pltpu.VMEM((4, 2, 32, 1024), BF),
            pltpu.VMEM((4, 2, 2, 32, 1024), BF),
            pltpu.VMEM((4, 2, 2, 64, 256), BF),
            pltpu.VMEM((2, 4, 64, 256), BF),
            pltpu.VMEM((2, 4, 4, 64, 256), BF),
            pltpu.VMEM((2, 4, 4, 64, 256), BF),
            pltpu.VMEM((2, 2, 2, 4, 4, 64, 256), BF),
            pltpu.VMEM((2, 2, 2, 4, 784, 128), BF),
            pltpu.VMEM((2, 2, 2, 4, 784, 128), BF),
            pltpu.VMEM((2, 2, 128, 128), BF),
            pltpu.VMEM((2, 2, 128, 128), BF),
            pltpu.VMEM((2, 2, 2, 4, 64, 1024), BF),
            pltpu.VMEM((2, 2, 2, 4, 4, 64, 256), BF),
            pltpu.VMEM((2, 2, 2, 4, 4, 64, 256), BF),
            pltpu.VMEM((2, 2, 4, 64, 256), BF),
            pltpu.VMEM((4, 2, 64, 256), BF),
            dma((10,)),
            dma((2,)), dma((2,)),
            dma((5,)), dma((3, 3, 2, 4)),
            dma((5,)), dma((5,)),
            dma((1,)), dma((2,)),
            dma((1,)), dma((2,)),
            dma((1,)), dma((2,)),
            dma((1,)), dma((2, 2)),
            dma((1,)), dma((2, 2)),
            dma((1,)), dma((2, 2)),
            dma((1,)), dma((2, 2)),
            dma((2,)), dma((2,)),
        ],
        compiler_params=pltpu.CompilerParams(
            collective_id=0, has_side_effects=True, vmem_limit_bytes=62 * 2**20
        ),
        cost_estimate=pl.CostEstimate(flops=11 * 10**9, bytes_accessed=20 * 10**6, transcendentals=10**6),
        name="decoder",
    )(text_embeds, patches, image_tokens, connector, w_query, w_keyval, w_out, cosine, sine)


def solution(mesh):
    placed = (
        P("dp", None, "tensor"),
        P("dp", "pipe", None),
        P("dp"),
        P("dp", "tensor"),
        P("pipe", "dp", "tensor"),
        P("pipe", None, "dp", "tensor"),
        P("pipe", "tensor", "dp"),
    )
    return jax.shard_map(
        shards, mesh=mesh, in_specs=placed, out_specs=P("dp", "pipe", "tensor"), check_vma=False
    )
```

```python
import math

import jax
import jax.numpy as jnp
import numpy as np
from jax import lax
from jax.experimental import pallas as pl
from jax.experimental.pallas import tpu as pltpu
from jax.sharding import PartitionSpec as P

MESH = pl.DeviceIdType.MESH
BF = jnp.bfloat16
F32 = jnp.float32
NX, NY, NZ = 4, 4, 8
SCALE = 1.0 / math.sqrt(128)
FAR_FIRST = (2, 1, 3)

RING = [
    (0, 2), (0, 3), (0, 4), (1, 2), (1, 3), (1, 4), (2, 1), (2, 2), (2, 3), (3, 1), (2, 4),
    (3, 2), (3, 3), (4, 1), (3, 4), (4, 2), (4, 3), (4, 4),
]
PIECES = (
    ((0, 16), (16, 16), (32, 32), (64, 16), (80, 16), (96, 16)),
    ((0, 32), (32, 32), (64, 32), (96, 32)),
    ((0, 512), (512, 512)),
)
WHOLE = (112, 128, 1024)

PROJECT, ATTEND, UPDATE, RENEW = range(4)
CODES = (
    1, 0, 2, 8, 9, 3, 16, 10, 17, 24, 11, 25, 18, 4, 19, 5, 26, 27, 12, 6, 13, 20, 7, 21, 14, 15, 22, 23, 28, 29, 30, 31,
)
AWAITED = {8 * PROJECT: 1, 8 * PROJECT + 4: 3, 8 * UPDATE: 2, 8 * UPDATE + 4: 4}
FIRST = {item: min(n for n, code in enumerate(CODES) if code // 4 == at // 4) for at, item in AWAITED.items()}
WORDS = [sum(code << (5 * n) for n, code in enumerate(CODES[i : i + 4])) for i in range(0, 32, 4)]


def remote(src, dst, send_sem, recv_sem, device):
    return pltpu.make_async_remote_copy(
        src_ref=src,
        dst_ref=dst,
        send_sem=send_sem,
        recv_sem=recv_sem,
        device_id=device,
        device_id_type=MESH,
    )


def kernel(
    text_in, patches_in, tokens_in, conn_in, wq, wkv, wo, cosine_in, sine_in, out,
    text, patches, tokens, conn, cosine, sine,
    CN, WQ, WO, PNS, PN, TS, T0, IS, IR, H, QS, QR, KS, VS, AR, OS, OR, FS, FR,
    l_s, own_s, own_r, z_s, z_r, f_s, f_r, p_s, p_r, t_s, t_r, i_s, i_r,
    h_s, h_r, q_s, q_r, a_s, a_r, o_s, o_r, e_s, e_r,
):
    c = lax.axis_index("pipe")
    d = lax.axis_index("dp")
    y = lax.axis_index("tensor")
    z = lax.div(d, NX)
    x = lax.rem(d, NX)

    def at(core, zz, xx, yy):
        return (core, zz * NX + xx, yy)

    def xk(k):
        return lax.rem(x + k, NX)

    def yk(k):
        return lax.rem(y + k, NY)

    def zk(k):
        return lax.rem(z + k + NZ, NZ)

    zrow = pl.multiple_of(z * 128, 128)
    local = [
        (conn_in, conn),
        (wq.at[0], WQ.at[c, pl.ds(zrow, 128), pl.ds(0, 1024)]),
        (wkv.at[0, 0], WQ.at[c, pl.ds(zrow, 128), pl.ds(1024, 256)]),
        (wkv.at[0, 1], WQ.at[c, pl.ds(zrow, 128), pl.ds(1280, 256)]),
        (patches_in, patches),
        (tokens_in, tokens),
        (text_in, text),
        (wo.at[0], WO.at[c, :, pl.ds(zrow, 128)]),
        (cosine_in, cosine),
        (sine_in, sine),
    ]
    loads = [pltpu.make_async_copy(a, b, l_s.at[n]) for n, (a, b) in enumerate(local)]
    for load in loads:
        load.start()

    barrier = pltpu.get_barrier_semaphore()
    both = [at(1 - c, z, xk(k), y) for k in range(4)] + [at(1 - c, zk(way), x, y) for way in (1, -1)]
    plane = [at(0, z, xk(k), y) for k in range(1, 4)] + [at(0, z, x, yk(k)) for k in range(1, 4)]
    line = [at(1, zk(way), x, y) for way in (1, -1)]

    def greet(devices):
        for device in devices:
            pl.semaphore_signal(barrier, inc=1, device_id=device, device_id_type=MESH)

    greet(both)

    @pl.when(c == 0)
    def _():
        greet(plane)
        pl.semaphore_wait(barrier, len(both) + len(plane))

    @pl.when(c == 1)
    def _():
        greet(line)
        pl.semaphore_wait(barrier, len(both) + len(line))

    loads[0].wait()
    CN[z, pl.ds(0, 96)] = conn[pl.ds(0, 96)]
    CN[z, pl.ds(96, 16)] = jnp.zeros((16, 1024), BF)
    CN[z, pl.ds(96, 4)] = conn[pl.ds(96, 4)]

    def kind(item):
        return 0 if item == 0 else 2 - item % 2

    def rows_of(item, zz, start, size):
        s = (item - 1) // 2
        if item == 0:
            return CN.at[zz, pl.ds(start, size)]
        if item % 2 == 1:
            return WQ.at[s, pl.ds(pl.multiple_of(zz * 128 + start, 32), size)]
        return WO.at[s, pl.ds(start, size), pl.ds(pl.multiple_of(zz * 128, 128), 128)]

    def block(item, zz):
        return rows_of(item, zz, 0, WHOLE[kind(item)])

    def own_copy(s, n):
        ref = block(1 + 2 * s + n, z)
        return remote(ref, ref, own_s.at[n], own_r.at[n], at(1 - s, z, x, y))

    def piece_ways(item, step):
        count = len(PIECES[kind(item)])
        return [(p, w) for p in range(count) for w in range(2) if step < 4 or p // (count // 2) == w]

    def piece_copy(item, step, piece, way, arriving):
        hops = step if arriving else step - 1
        zz = zk(-hops) if way == 0 else zk(hops)
        ref = rows_of(item, zz, *PIECES[kind(item)][piece])
        target = at(1 if step < 4 else 0, zk(1) if way == 0 else zk(-1), x, y)
        arrived = z_r.at[item % 3, step - 1, way, piece] if step < 4 else f_r.at[item]
        return remote(ref, ref, z_s.at[item], arrived, target)

    def blocks(item, count):
        s = (item - 1) // 2
        if item == 0:
            return CN.at[pl.ds(0, count), pl.ds(0, 112)]
        if item % 2 == 1:
            return WQ.at[s, pl.ds(0, 128 * count)]
        return WO.at[s, :, pl.ds(0, 128 * count)]

    def waits(ref, semaphore):
        return remote(ref, ref, semaphore, semaphore, at(1 - c, z, x, y))

    def hand_over(item, index):
        step = index // 2 + 1
        zz = zk(-step) if index % 2 == 0 else zk(step)
        ref = block(item, zz)
        return remote(ref, ref, f_s.at[item], f_r.at[item], at(0, z, x, y))

    def patch_copy(k):
        return remote(PNS.at[xk(k)], PN.at[x, :, c], p_s.at[0], p_r.at[c], at(0, z, xk(k), y))

    def normed_patches():
        values = patches[...].reshape(64, 3200).astype(F32)
        centered = values - jnp.sum(values, axis=-1, keepdims=True) / 3200.0
        variance = jnp.sum(centered * centered, axis=-1, keepdims=True) / 3200.0
        normed = centered * lax.rsqrt(variance + 1e-06)
        row = lax.broadcasted_iota(jnp.int32, (64, 1), 0)
        limit = jnp.where(row < 32, tokens[0], tokens[1])
        normed = jnp.where(c * 32 + lax.rem(row, 32) < limit, normed, 0.0)
        lane = lax.broadcasted_iota(jnp.int32, (64, 128), 1)
        for j in range(32):
            zz, xx = divmod(j, NX)
            base = (100 * j) // 128 * 128
            offset = 100 * j - base
            width = 128 if offset + 100 <= 128 else 256
            window = normed[:, base : base + width]
            if offset:
                window = pltpu.roll(window, width - offset, 1)
            part = jnp.where(lane < 100, window[:, :128], 0.0)
            PNS[xx, :, :, zz * 128 : (zz + 1) * 128] = part.astype(BF).reshape(2, 32, 128)

    @pl.when(c == 1)
    def _():
        for piece, way in piece_ways(0, 1):
            piece_copy(0, 1, piece, way, False).start()
        for load in loads[1:]:
            load.wait()
        own = [own_copy(1, 0), own_copy(1, 1)]
        for copy in own:
            copy.start()
        normed_patches()
        for k in range(4):
            patch_copy(k).start()
        own_copy(0, 0).wait_recv()
        for way in range(2):
            piece_copy(1, 1, 0, way, False).start()
        for item, step in RING:
            if step == 1:
                if item == 2:
                    own_copy(0, 1).wait_recv()
                for piece, way in piece_ways(item, 1):
                    piece_copy(item, 1, piece, way, False).start()
            else:
                onward = piece_ways(item, step)
                for piece, way in piece_ways(item, step - 1):
                    piece_copy(item, step - 1, piece, way, True).wait_recv()
                    if (piece, way) in onward:
                        piece_copy(item, step, piece, way, False).start()
                if item == 0:
                    for way in range(2):
                        piece_copy(1, 1, step - 1, way, False).start()
                for index in (2 * step - 4, 2 * step - 3):
                    hand_over(item, index).start()
        for copy in own:
            copy.wait_send()
        waits(PNS, p_s.at[0]).wait_send()
        for item in range(5):
            waits(blocks(item, 7), z_s.at[item]).wait_send()
            waits(blocks(item, 6), f_s.at[item]).wait_send()

    def wait_item(item):
        waits(blocks(item, 7), f_r.at[item]).wait_recv()

    def text_copy(half, k):
        target = at(0, z, xk(k), y)
        if half == 1:
            return remote(TS.at[xk(k), :, 1], H.at[0, :, 1, y, x], t_s.at[0], t_r.at[1], target)
        return remote(TS.at[xk(k), :, 0], T0.at[:, x], t_s.at[0], t_r.at[0], target)

    def text_arrival(half):
        waits(H.at[0, :, 1, y, pl.ds(0, 3)] if half == 1 else T0.at[:, pl.ds(0, 3)], t_r.at[half]).wait_recv()

    def image_copy(b, k):
        return remote(IS.at[b, xk(k)], IR.at[b, x], i_s.at[0], i_r.at[b], at(0, z, xk(k), y))

    def image_arrival(b):
        waits(IR.at[b, pl.ds(0, 3)], i_r.at[b]).wait_recv()

    def hidden_copy(s, b, h, k):
        ref = H.at[s, b, h, y]
        return remote(ref, ref, h_s.at[0], h_r.at[b, h], at(0, z, x, yk(k)))

    def hidden_arrival(s, b, h):
        waits(H.at[s, b, h, pl.ds(0, 3)], h_r.at[b, h]).wait_recv()

    def qkv_copy(s, b, h, k, part):
        rows = pl.ds(0, 256) if part == 0 else pl.ds(256, 528)
        return remote(
            QS.at[s, b, h, xk(k), rows], QR.at[s, b, h, x, rows], q_s.at[0], q_r.at[b, h], at(0, z, xk(k), y)
        )

    def qkv_arrival(s, b, h):
        waits(QR.at[s, b, h, pl.ds(0, 3)], q_r.at[b, h]).wait_recv()

    def attended_copy(s, b, h, k, g):
        ref = AR.at[s, b, h, x, :, pl.ds(g * 512, 512)]
        return remote(ref, ref, a_s.at[0], a_r.at[b, h], at(0, z, xk(k), y))

    def attended_arrival(s, b, h):
        waits(AR.at[s, b, h, pl.ds(0, 3)], a_r.at[b, h]).wait_recv()

    def update_copy(s, b, h, k):
        return remote(OS.at[s, b, h, yk(k)], OR.at[s, b, h, y], o_s.at[0], o_r.at[b, h], at(0, z, x, yk(k)))

    def update_arrival(s, b, h):
        waits(OR.at[s, b, h, pl.ds(0, 3)], o_r.at[b, h]).wait_recv()

    def final_copy(b, h, k):
        return remote(FS.at[b, h, xk(k)], FR.at[x, b], e_s.at[h], e_r.at[b], at(h, z, xk(k), y))

    def send_text():
        position = lax.broadcasted_iota(jnp.int32, (128, 1), 0)
        for b in range(2):
            masked = jnp.where(position < tokens[b], jnp.zeros_like(text[b]), text[b])
            for xx in range(NX):
                for zz in range(2):
                    lanes = zz * 512 + xx * 128
                    TS[xx, b, :, :, zz * 128 : (zz + 1) * 128] = masked[:, lanes : lanes + 128].reshape(2, 64, 128)
        for b in range(2):
            H[0, b, 1, y, x] = TS[x, b, 1]
            T0[b, x] = TS[x, b, 0]
        for half in (1, 0):
            for k in FAR_FIRST:
                text_copy(half, k).start()

    def image_part():
        waits(PN.at[pl.ds(0, 3), :, 0], p_r.at[0]).wait_recv()
        waits(PN.at[:, :, 1], p_r.at[1]).wait_recv()
        wait_item(0)
        for b in range(2):
            rows = PN[:, b].reshape(256, 1024)
            for zz in range(2):
                for pair in range(2):
                    lanes = zz * 512 + pair * 256
                    product = jnp.dot(
                        rows, CN[:, :, lanes : lanes + 256].reshape(1024, 256), preferred_element_type=F32
                    ).astype(BF)
                    for n in range(2):
                        part = product[:, n * 128 : (n + 1) * 128]
                        IS[b, 2 * pair + n, :, :, zz * 128 : (zz + 1) * 128] = part.reshape(4, 64, 128)
            for k in FAR_FIRST:
                image_copy(b, k).start()
        text_arrival(0)
        for b in range(2):
            image_arrival(b)
            total = IS[b, x].astype(F32)
            for k in FAR_FIRST:
                total = total + IR[b, xk(k)].astype(F32)
            H[0, b, 0, y] = (total.astype(BF).astype(F32) + T0[b].astype(F32)).astype(BF)
            for k in FAR_FIRST:
                hidden_copy(0, b, 0, k).start()

    def project(s, b, h):
        squares = jnp.zeros((256, 256), F32)
        for q in range(4):
            values = H[s, b, h, q].reshape(256, 256).astype(F32)
            squares = squares + values * values
        squares = jnp.sum(squares, axis=-1, keepdims=True)
        high = squares.astype(BF).astype(F32)
        row = lax.rem(lax.broadcasted_iota(jnp.int32, (256, 128), 0), 64)
        lane = lax.broadcasted_iota(jnp.int32, (256, 128), 1)
        spread = jnp.where(lane == row, high, jnp.where(lane == row + 64, squares - high, 0.0))
        spread = jnp.sum(spread.reshape(4, 64, 128), axis=1, keepdims=True)
        QS[s, b, h, :, 768:784, :] = jnp.broadcast_to(spread, (4, 16, 128)).astype(BF)

        def tile(n, _):
            lanes = pl.ds(pl.multiple_of(n * 256, 256), 256)
            total = jnp.zeros((256, 256), F32)
            for q in range(4):
                total = total + jnp.dot(
                    H[s, b, h, q].reshape(256, 256),
                    WQ[s, pl.ds(q * 256, 256), lanes],
                    preferred_element_type=F32,
                )
            for i in range(2):
                rows = pl.ds(pl.multiple_of((2 * n + i) * 64, 64), 64)
                QS[s, b, h, :, rows, :] = total[:, i * 128 : (i + 1) * 128].astype(BF).reshape(4, 64, 128)

            @pl.when(n == 1)
            def _():
                for k in FAR_FIRST:
                    qkv_copy(s, b, h, k, 0).start()

            return 0

        lax.fori_loop(0, 6, tile, 0)
        for k in FAR_FIRST:
            qkv_copy(s, b, h, k, 1).start()

    def attend(s, b, h):
        qkv_arrival(s, b, h)

        def summed(start, size=64):
            rows = slice(start, start + size)
            total = QS[s, b, h, x, rows].astype(F32)
            for k in FAR_FIRST:
                total = total + QR[s, b, h, xk(k), rows].astype(F32)
            return total

        row = lax.broadcasted_iota(jnp.int32, (64, 128), 0)
        lane = lax.broadcasted_iota(jnp.int32, (64, 128), 1)
        spread = jnp.where(lax.rem(lane, 64) == row, summed(768, 16)[0:1], 0.0)
        squares = jnp.sum(spread, axis=-1, keepdims=True)
        scale = lax.rsqrt(squares / 4096.0 + 1e-05)
        half = pl.ds(pl.multiple_of(h * 64, 64), 64)
        cos_rows = cosine[half]
        sin_rows = sine[half]

        def rotated(start):
            rows = summed(start) * scale
            return (rows * cos_rows + pltpu.roll(rows, 64, 1) * sin_rows).astype(BF)

        row = lax.rem(lax.broadcasted_iota(jnp.int32, (256, 128), 0), 64) + h * 64
        column = lax.broadcasted_iota(jnp.int32, (256, 128), 1)
        for g in range(2):
            KS[b, g, half] = rotated((8 + g) * 64)
            VS[b, g, half] = (summed((10 + g) * 64) * scale).astype(BF)
            stacked = jnp.concatenate([rotated((4 * g + j) * 64) for j in range(4)], axis=0)
            scores = lax.dot_general(
                stacked, KS[b, g], (((1,), (1,)), ((), ())), preferred_element_type=F32
            )
            scores = jnp.where(row >= column, scores * SCALE, -1e30)
            weights = jnp.exp(scores - jnp.max(scores, axis=-1, keepdims=True))
            norm = jnp.sum(weights, axis=-1, keepdims=True)
            mixed = jnp.dot(weights.astype(BF), VS[b, g], preferred_element_type=F32) / norm
            for j in range(4):
                lanes = (4 * g + j) * 128
                AR[s, b, h, x, :, lanes : lanes + 128] = mixed[j * 64 : (j + 1) * 64].astype(BF)
            for k in FAR_FIRST:
                attended_copy(s, b, h, k, g).start()

    def update(s, b, h):
        attended_arrival(s, b, h)

        def tile(n, _):
            k = jnp.where(n == 0, 2, jnp.where(n == 1, 1, jnp.where(n == 2, 3, 0)))
            yd = yk(k)
            lanes = pl.ds(pl.multiple_of(yd * 256, 256), 256)
            product = jnp.dot(AR[s, b, h].reshape(256, 1024), WO[s, :, lanes], preferred_element_type=F32)
            OS[s, b, h, yd] = product.astype(BF).reshape(4, 64, 256)

            @pl.when(n < 3)
            def _():
                update_copy(s, b, h, k).start()

            return 0

        lax.fori_loop(0, 4, tile, 0)

    def renew(s, b, h):
        update_arrival(s, b, h)
        total = OS[s, b, h, y].astype(F32)
        for k in FAR_FIRST:
            total = total + OR[s, b, h, yk(k)].astype(F32)
        fresh = (H[s, b, h, y].astype(F32) + total).astype(BF)

        @pl.when(s == 0)
        def _():
            H[1, b, h, y] = fresh
            for k in FAR_FIRST:
                hidden_copy(1, b, h, k).start()

        @pl.when(s == 1)
        def _():
            FS[b, h] = fresh
            for k in FAR_FIRST:
                final_copy(b, h, k).start()

            @pl.when(h == 0)
            def _():
                FR[x, b] = FS[b, 0, x]

            @pl.when(h == 1)
            def _():
                final_copy(b, h, 0).start()

    @pl.when(c == 0)
    def _():
        for load in loads[1:4]:
            load.wait()
        own_copy(0, 0).start()
        for load in loads[4:]:
            load.wait()
        own_copy(0, 1).start()
        send_text()
        for zz in range(NZ):
            CN[zz, pl.ds(112, 16)] = jnp.zeros((16, 1024), BF)
        KS[...] = jnp.zeros_like(KS)
        VS[...] = jnp.zeros_like(VS)
        normed_patches()
        PN[x, :, 0] = PNS[x]
        for k in FAR_FIRST:
            patch_copy(k).start()
        text_arrival(1)
        for b in range(2):
            for k in FAR_FIRST:
                hidden_copy(0, b, 1, k).start()
        image_part()

        def stage(n, word):
            fresh = jnp.int32(WORDS[7])
            for m in range(7):
                fresh = jnp.where(lax.div(n, 4) == m, jnp.int32(WORDS[m]), fresh)
            word = jnp.where(lax.rem(n, 4) == 0, fresh, word)
            code = lax.rem(word, 32)
            what = lax.div(code, 8)
            s = lax.rem(lax.div(code, 4), 2)
            b = lax.rem(lax.div(code, 2), 2)
            h = lax.rem(code, 2)

            for item in range(1, 5):

                @pl.when(n == FIRST[item])
                def _():
                    if item > 2:
                        own_copy(1, item - 3).wait_recv()
                    wait_item(item)

            @pl.when(what == PROJECT)
            def _():
                hidden_arrival(s, b, h)
                project(s, b, h)

            @pl.when(what == ATTEND)
            def _():
                attend(s, b, h)

            @pl.when(what == UPDATE)
            def _():
                update(s, b, h)

            @pl.when(what == RENEW)
            def _():
                renew(s, b, h)

            return lax.div(word, 32)

        lax.fori_loop(0, 32, stage, jnp.int32(0))

    for b in range(2):

        @pl.when(c == 0)
        def _():
            waits(FR.at[pl.ds(0, 3), b], e_r.at[b]).wait_recv()

        @pl.when(c == 1)
        def _():
            waits(FR.at[:, b], e_r.at[b]).wait_recv()

    for b in range(2):
        for xx in range(NX):
            for zz in range(2):
                lanes = zz * 512 + xx * 128
                out[b, :, lanes : lanes + 128] = FR[xx, b, :, zz * 128 : (zz + 1) * 128]

    @pl.when(c == 0)
    def _():
        own_copy(0, 0).wait_send()
        own_copy(0, 1).wait_send()
        waits(PNS.at[pl.ds(0, 3)], p_s.at[0]).wait_send()
        waits(TS.at[pl.ds(0, 3)], t_s.at[0]).wait_send()
        waits(IS.at[:, pl.ds(0, 3)], i_s.at[0]).wait_send()
        for sent, semaphore in ((H, h_s), (QS, q_s), (AR, a_s), (OS, o_s)):
            waits(sent.at[:, :, :, pl.ds(0, 3)], semaphore.at[0]).wait_send()
        waits(FS.at[:, 0, pl.ds(0, 3)], e_s.at[0]).wait_send()
        waits(FS.at[:, 1], e_s.at[1]).wait_send()


def rotation_tables():
    frequencies = 500000.0 ** (-(np.arange(64, dtype=np.float32) * np.float32(2.0) / np.float32(128)))
    angles = np.arange(128, dtype=np.float32)[:, None] * frequencies.astype(np.float32)[None, :]
    cosine, sine = np.cos(angles), np.sin(angles)
    return (
        np.concatenate([cosine, cosine], axis=1).astype(np.float32),
        np.concatenate([-sine, sine], axis=1).astype(np.float32),
    )


def shards(text_embeds, patches, image_tokens, connector, w_query, w_keyval, w_out):
    cosine, sine = rotation_tables()
    vmem = pl.BlockSpec(memory_space=pltpu.VMEM)
    dma = pltpu.SemaphoreType.DMA
    return pl.pallas_call(
        kernel,
        out_shape=jax.ShapeDtypeStruct((2, 64, 1024), BF),
        in_specs=[pl.BlockSpec(memory_space=pl.ANY)] * 9,
        out_specs=vmem,
        scratch_shapes=[
            pltpu.VMEM((2, 128, 1024), BF),
            pltpu.VMEM((2, 32, 3200), BF),
            pltpu.SMEM((2,), jnp.int32),
            pltpu.VMEM((100, 1024), BF),
            pltpu.VMEM((128, 128), F32),
            pltpu.VMEM((128, 128), F32),
            pltpu.VMEM((8, 128, 1024), BF),
            pltpu.VMEM((2, 1024, 1536), BF),
            pltpu.VMEM((2, 1024, 1024), BF),
            pltpu.VMEM((4, 2, 32, 1024), BF),
            pltpu.VMEM((4, 2, 2, 32, 1024), BF),
            pltpu.VMEM((4, 2, 2, 64, 256), BF),
            pltpu.VMEM((2, 4, 64, 256), BF),
            pltpu.VMEM((2, 4, 4, 64, 256), BF),
            pltpu.VMEM((2, 4, 4, 64, 256), BF),
            pltpu.VMEM((2, 2, 2, 4, 4, 64, 256), BF),
            pltpu.VMEM((2, 2, 2, 4, 784, 128), BF),
            pltpu.VMEM((2, 2, 2, 4, 784, 128), BF),
            pltpu.VMEM((2, 2, 128, 128), BF),
            pltpu.VMEM((2, 2, 128, 128), BF),
            pltpu.VMEM((2, 2, 2, 4, 64, 1024), BF),
            pltpu.VMEM((2, 2, 2, 4, 4, 64, 256), BF),
            pltpu.VMEM((2, 2, 2, 4, 4, 64, 256), BF),
            pltpu.VMEM((2, 2, 4, 64, 256), BF),
            pltpu.VMEM((4, 2, 64, 256), BF),
            dma((10,)),
            dma((2,)), dma((2,)),
            dma((5,)), dma((3, 3, 2, 6)),
            dma((5,)), dma((5,)),
            dma((1,)), dma((2,)),
            dma((1,)), dma((2,)),
            dma((1,)), dma((2,)),
            dma((1,)), dma((2, 2)),
            dma((1,)), dma((2, 2)),
            dma((1,)), dma((2, 2)),
            dma((1,)), dma((2, 2)),
            dma((2,)), dma((2,)),
        ],
        compiler_params=pltpu.CompilerParams(
            collective_id=0, has_side_effects=True, vmem_limit_bytes=62 * 2**20
        ),
        cost_estimate=pl.CostEstimate(flops=11 * 10**9, bytes_accessed=20 * 10**6, transcendentals=10**6),
        name="decoder",
    )(text_embeds, patches, image_tokens, connector, w_query, w_keyval, w_out, cosine, sine)


def solution(mesh):
    placed = (
        P("dp", None, "tensor"),
        P("dp", "pipe", None),
        P("dp"),
        P("dp", "tensor"),
        P("pipe", "dp", "tensor"),
        P("pipe", None, "dp", "tensor"),
        P("pipe", "tensor", "dp"),
    )
    return jax.shard_map(
        shards, mesh=mesh, in_specs=placed, out_specs=P("dp", "pipe", "tensor"), check_vma=False
    )
```
